128 devices in a mesh: batch: 8 (over y, core), frame: 16 (over x, z).
Axes of the slice: x: 4, y: 4, z: 4, core: 2. Of those that a mesh axis runs over, the one named last changes fastest.
Arguments:
- tokens: bfloat16 [8, 32, 256, 1408], P('batch', 'frame'), may hold values from -6 to 6
- frame_time: int32 [8, 32], P('batch'), may hold values from 0 to 31, each once within a row
- valid_count: int32 [8], P('batch'), may hold values from 8 to 32, as said below
- spatial_qkv: bfloat16 [1408, 2112], replicated, may hold values from -0.15625 to 0.15625
- spatial_out: bfloat16 [704, 1408], replicated, may hold values from -0.21875 to 0.21875
- temporal_qkv: bfloat16 [1408, 2112], replicated, may hold values from -0.15625 to 0.15625
- temporal_out: bfloat16 [704, 1408], replicated, may hold values from -0.21875 to 0.21875
- time_embed: float32 [32, 1408], replicated, may hold values from -6 to 6
- video_proj: bfloat16 [1408, 512], replicated, may hold values from -0.15625 to 0.15625
- text_embed: float32 [8, 512], P('batch'), may hold values from -6 to 6
Outputs:
- grad_tokens: bfloat16 [8, 32, 256, 1408], P('batch', 'frame')
- loss: float32 [], replicated
The draws below stay inside these ranges and needn't reach their ends.
Inputs may be any that keep to these rules, and one draw needn't show every extreme that they name: `frame_time`: each row is a permutation of the time indices 0 to 31. `valid_count`: some clip has all 32 frames valid and another has 8.
All inputs are finite; a program needn't handle non-finite values.
Results may differ from the reference program's by a relative error of at most 0.015.
Values may be sent and summed in bfloat16 or wider, within the bound.
No kernel may reach another device: no remote copies, remote signals or barrier semaphores. Data moves between devices by JAX's collectives and lax.ppermute only.
A program may use at most 128 MiB of HBM per device.

```python
import math
import jax
import jax.numpy as jnp
from jax import lax

D = 1408
HEADS = 8
HD = 88
INNER = 704
PATCHES = 256
EMBED = 512
FR = 32
CLIPS = 8


def draw_tokens(key, part):
    key = jax.random.fold_in(key, 11)
    key_patch, key_frame = jax.random.split(key, 2)
    patch_values = jax.random.normal(key_patch, (CLIPS, FR, PATCHES, D), jnp.float32)
    frame_shift = 1.5 * jax.random.normal(key_frame, (CLIPS, FR, 1, D), jnp.float32)
    return jnp.clip(patch_values + frame_shift, -6.0, 6.0).astype(jnp.bfloat16)


def draw_valid_count(key, part):
    key = jax.random.fold_in(key, 7)
    key_counts, key_place = jax.random.split(key, 2)
    counts = jax.random.randint(key_counts, (CLIPS,), FR // 4, FR + 1)
    full_at = jax.random.randint(key_place, (), 0, CLIPS)
    clip_slots = jnp.arange(CLIPS)
    counts = jnp.where(clip_slots == full_at, FR, counts)
    counts = jnp.where(clip_slots == (full_at + 1) % CLIPS, FR // 4, counts)
    return counts.astype(jnp.int32)


def levels(rng, shape, pieces, least, high):
    gain = 1.0
    for position, blocks in pieces:
        heights = jax.random.uniform(jax.random.fold_in(jax.random.fold_in(rng, 6), position), (blocks,), jnp.float32, least / len(pieces), high / len(pieces))
        gain = gain * jnp.repeat(jnp.exp(heights), shape[position] // blocks).reshape((-1,) + (1,) * (len(shape) - 1 - position))
    return gain


def bell_draw(own_key, dims, scale, reach, shards=(), held_as=jnp.bfloat16):
    array = scale * jax.random.normal(own_key, dims, jnp.float32)
    if shards:
        array = array * levels(own_key, dims, shards, -0.22, 0.18)
    return jnp.clip(array, -reach, reach).astype(held_as)


def setup_inputs(seed: int = 0) -> dict:
    key_of = jax.random.split(jax.random.key(seed), 11)
    tokens = draw_tokens(jax.random.fold_in(key_of[10], 71), 0)
    frame_time = jax.vmap(lambda own: jax.random.permutation(own, FR))(jax.random.split(key_of[1], CLIPS)).reshape((CLIPS, FR)).astype(jnp.int32)
    valid_count = draw_valid_count(jax.random.fold_in(key_of[10], 71), 0)
    spatial_qkv = bell_draw(key_of[3], (D, 3 * INNER), D ** -0.5, 0.15625)
    spatial_out = bell_draw(key_of[4], (INNER, D), INNER ** -0.5, 0.21875)
    temporal_qkv = bell_draw(key_of[5], (D, 3 * INNER), D ** -0.5, 0.15625)
    temporal_out = bell_draw(key_of[6], (INNER, D), INNER ** -0.5, 0.21875)
    time_embed = bell_draw(key_of[7], (FR, D), 1.0, 6.0, (), jnp.float32)
    video_proj = bell_draw(key_of[8], (D, EMBED), D ** -0.5, 0.15625)
    text_embed = bell_draw(key_of[9], (CLIPS, EMBED), 1.0, 6.0, ((0, 8),), jnp.float32)
    return dict(tokens=tokens, frame_time=frame_time, valid_count=valid_count, spatial_qkv=spatial_qkv, spatial_out=spatial_out, temporal_qkv=temporal_qkv, temporal_out=temporal_out, time_embed=time_embed, video_proj=video_proj, text_embed=text_embed)


epsilon = 1e-06
sharpness_scale = 1.0 / 0.07

def layer_norm(values):
    center = values - lax.optimization_barrier(jnp.mean(values, axis=-1, keepdims=True))
    spread = lax.optimization_barrier(jnp.mean(center * center, axis=-1, keepdims=True))
    return center / jnp.sqrt(spread + epsilon)

def split_heads(packed, which_part):
    section = packed[..., which_part * HEADS * HD:(which_part + 1) * HEADS * HD]
    return section.reshape(section.shape[:-1] + (HEADS, HD)).astype(jnp.float32)

def spatial_layer(frames_in, spatial_qkv, spatial_out):
    normed = layer_norm(frames_in.astype(jnp.float32)).astype(jnp.bfloat16)
    packed = jnp.dot(normed, spatial_qkv, preferred_element_type=jnp.float32).astype(jnp.bfloat16)
    queries = split_heads(packed, 0)
    key_heads = split_heads(packed, 1)
    value_heads = split_heads(packed, 2)
    scores = jnp.einsum('fqhd,fkhd->fhqk', queries, key_heads) / math.sqrt(HD)
    raised = jnp.exp(scores)
    weights = (raised / lax.optimization_barrier(jnp.sum(raised, axis=-1, keepdims=True))).astype(jnp.bfloat16)
    mixture = jnp.einsum('fhqk,fkhd->fqhd', weights.astype(jnp.float32), value_heads)
    mixture = mixture.reshape(mixture.shape[:2] + (HEADS * HD,)).astype(jnp.bfloat16)
    update = jnp.dot(mixture, spatial_out, preferred_element_type=jnp.float32)
    return (frames_in.astype(jnp.float32) + update).astype(jnp.bfloat16)

def temporal_front(frames_x1, time_embed, frame_times, temporal_qkv):
    lookup = (frame_times[:, None] == jnp.arange(time_embed.shape[0], dtype=jnp.int32)[None, :]).astype(jnp.float32)
    rows_added = jnp.dot(lookup, time_embed, precision=lax.Precision.HIGHEST)
    shifted = frames_x1.astype(jnp.float32) + rows_added[:, None, :]
    normed = layer_norm(shifted).astype(jnp.bfloat16)
    packed = jnp.dot(normed, temporal_qkv, preferred_element_type=jnp.float32).astype(jnp.bfloat16)
    return (shifted, packed)

def temporal_core(packed, valid_mask):
    queries = split_heads(packed, 0)
    key_heads = split_heads(packed, 1)
    value_heads = split_heads(packed, 2)
    scores = jnp.einsum('qphd,kphd->phqk', queries, key_heads) / math.sqrt(HD)
    raised = jnp.exp(scores) * valid_mask[None, None, None, :]
    weights = (raised / lax.optimization_barrier(jnp.sum(raised, axis=-1, keepdims=True))).astype(jnp.bfloat16)
    mixture = jnp.einsum('phqk,kphd->qphd', weights.astype(jnp.float32), value_heads)
    return jnp.einsum('q,qphd->hd', valid_mask, mixture).reshape(HEADS * HD)

def pool_rows(shifted, valid_mask):
    return lax.optimization_barrier(jnp.sum(shifted * valid_mask[:, None, None], axis=(0, 1)))

def finish_embed(rows_total, mixed_total, clip_count, temporal_out, video_proj, patches):
    through = jnp.dot(mixed_total, temporal_out.astype(jnp.float32), precision=lax.Precision.HIGHEST)
    feature = (rows_total + through) / (clip_count.astype(jnp.float32) * patches)
    return jnp.dot(feature, video_proj.astype(jnp.float32), precision=lax.Precision.HIGHEST)

def unit_rows(matrix):
    return matrix / jnp.sqrt(lax.optimization_barrier(jnp.sum(matrix * matrix, axis=-1, keepdims=True)) + epsilon)

def pair_loss(video_vectors, text_vectors):
    pair_scores = jnp.dot(video_vectors, text_vectors.T, precision=lax.Precision.HIGHEST) * sharpness_scale
    raised = jnp.exp(pair_scores)
    row_part = jnp.sum(jnp.log(lax.optimization_barrier(jnp.sum(raised, axis=1))))
    column_part = jnp.sum(jnp.log(lax.optimization_barrier(jnp.sum(raised, axis=0))))
    return 0.5 * (row_part + column_part) - jnp.sum(jnp.diagonal(pair_scores))

def reference(tokens, frame_time, valid_count, spatial_qkv, spatial_out, temporal_qkv, temporal_out, time_embed, video_proj, text_embed):

    def embed_clip(frames_in, frame_times, clip_count):
        frames_x1 = spatial_layer(frames_in, spatial_qkv, spatial_out)
        valid_mask = (frame_times < clip_count).astype(jnp.float32)
        shifted, packed = temporal_front(frames_x1, time_embed, frame_times, temporal_qkv)
        rows_total = pool_rows(shifted, valid_mask)
        mixed_total = temporal_core(packed, valid_mask)
        return finish_embed(rows_total, mixed_total, clip_count, temporal_out, video_proj, frames_in.shape[1])

    def forward_one(bundle):
        return embed_clip(bundle[0], bundle[1], bundle[2])
    projected = lax.map(forward_one, (tokens, frame_time, valid_count))
    text_vectors = unit_rows(text_embed)
    loss_value, loss_back = jax.vjp(lambda matrix: pair_loss(unit_rows(matrix), text_vectors), projected)
    random_start = jnp.asarray(FR * PATCHES, dtype=loss_value.dtype)
    cotangent = loss_back(random_start)[0]

    def backward_one(bundle):
        frames_in, frame_times, clip_count, grad_row = bundle
        unused, back_fn = jax.vjp(lambda values: embed_clip(values, frame_times, clip_count), frames_in)
        return back_fn(grad_row)[0]
    grad_tokens = lax.map(backward_one, (tokens, frame_time, valid_count, cotangent))
    return (grad_tokens, loss_value)
```

```python
import functools
import math

import jax
import jax.numpy as jnp
from jax import lax
from jax.experimental import pallas as pl
from jax.experimental.pallas import tpu as pltpu
from jax.sharding import PartitionSpec as P

HEADS = 8
HD = 88
INNER = HEADS * HD
LANES = 128
GROUP = 8
EPSILON = 1e-06
SHARPNESS = 1.0 / 0.07
SCALE = 1.0 / math.sqrt(HD)
MIB = 1024 * 1024

bf16 = jnp.bfloat16
f32 = jnp.float32
VMEM = pl.BlockSpec(memory_space=pltpu.VMEM)
HBM = pl.BlockSpec(memory_space=pltpu.HBM)


def dot_nn(left, right):
    return lax.dot_general(left, right, (((1,), (0,)), ((), ())), preferred_element_type=f32)


def dot_nt(left, right):
    return lax.dot_general(left, right, (((1,), (1,)), ((), ())), preferred_element_type=f32)


def dot_tn(left, right):
    return lax.dot_general(left, right, (((0,), (0,)), ((), ())), preferred_element_type=f32)


def split_terms(values, terms):
    parts = []
    rest = values
    for _ in range(terms):
        part = rest.astype(bf16)
        parts.append(part)
        rest = rest - part.astype(f32)
    return parts


def exact(dot, values, matrix, terms=3):
    rows = values.shape[0]
    products = dot(jnp.concatenate(split_terms(values, terms), axis=0), matrix)
    total = products[:rows]
    for term in range(1, terms):
        total = total + products[term * rows : (term + 1) * rows]
    return total


def window(head):
    first = head * HD // LANES * LANES
    last = min(-(-(head + 1) * HD // LANES) * LANES, INNER)
    return first, last, head * HD - first


def head_lanes(rows, head):
    first, last, offset = window(head)
    lane = lax.broadcasted_iota(jnp.int32, (rows, last - first), 1)
    return (lane >= offset) & (lane < offset + HD)


def keep_head(values, head):
    return jnp.where(head_lanes(values.shape[0], head), values, jnp.zeros_like(values))


def merge_heads(products):
    tiles = []
    for start in range(0, INNER, LANES):
        width = min(LANES, INNER - start)
        tile = None
        for head in range(HEADS):
            first, last, offset = window(head)
            if first <= start < last:
                piece = products[head][:, start - first : start - first + width]
                if tile is None:
                    tile = piece
                else:
                    lane = lax.broadcasted_iota(jnp.int32, piece.shape, 1)
                    tile = jnp.where(lane >= head * HD - start, piece, tile)
        tiles.append(tile)
    return jnp.concatenate(tiles, axis=1)


def normalize(values):
    center = values - jnp.mean(values, axis=-1, keepdims=True)
    spread = jnp.mean(center * center, axis=-1, keepdims=True)
    inverse = lax.rsqrt(spread + EPSILON)
    return center * inverse, inverse


def normalize_back(grad, normed, inverse):
    return inverse * (
        grad
        - jnp.mean(grad, axis=-1, keepdims=True)
        - normed * jnp.mean(grad * normed, axis=-1, keepdims=True)
    )


def spatial_norm(count_ref, tok_ref, xn_ref, inverse_ref, count_out_ref):
    count_out_ref[...] = count_ref[...]
    for frame in range(tok_ref.shape[0]):
        normed, inverse = normalize(tok_ref[frame].astype(f32))
        xn_ref[frame] = normed.astype(bf16)
        inverse_ref[frame] = inverse


def spatial_forward(tok_ref, xn_ref, qkv_ref, out_ref, x1_ref, q_ref, k_ref, v_ref, p_ref):
    frames, patches, _ = tok_ref.shape
    owners = x1_ref.shape[0]
    share = patches // owners
    for frame in range(frames):
        for i, held_ref in enumerate((q_ref, k_ref, v_ref)):
            part = qkv_ref[i * INNER : (i + 1) * INNER, :]
            held_ref[frame] = dot_nt(xn_ref[frame], part).astype(bf16)
        mixed = []
        for head in range(HEADS):
            first, last, _ = window(head)
            query = keep_head(q_ref[frame, :, first:last], head)
            raised = jnp.exp(dot_nt(query, k_ref[frame, :, first:last]) * SCALE)
            weights = (raised * (1.0 / jnp.sum(raised, axis=-1, keepdims=True))).astype(bf16)
            p_ref[frame, head] = weights
            mixed.append(dot_nn(weights, v_ref[frame, :, first:last]))
        update = dot_nn(merge_heads(mixed).astype(bf16), out_ref[...])
        x1 = (tok_ref[frame].astype(f32) + update).astype(bf16)
        own = slice(frame * share, (frame + 1) * share)
        x1_ref[:, own, :] = x1.reshape(owners, share, x1.shape[-1])


def spatial_backward(
    grad_ref,
    xn_ref,
    inverse_ref,
    qkv_ref,
    out_ref,
    q_ref,
    k_ref,
    v_ref,
    p_ref,
    result_hbm,
    result_ref,
    result_sem,
):
    frames, patches, width = xn_ref.shape
    owners = grad_ref.shape[0]
    share = patches // owners
    copies = []
    for frame in range(frames):
        own = slice(frame * share, (frame + 1) * share)
        grad_x1 = grad_ref[:, own, :].reshape(patches, width)
        grad_so = dot_nt(grad_x1, out_ref[...]).astype(bf16)
        dq, dk, dv = [], [], []
        for head in range(HEADS):
            first, last, _ = window(head)
            grad_head = grad_so[:, first:last]
            weights = p_ref[frame, head]
            grad_weights = dot_nt(keep_head(grad_head, head), v_ref[frame, :, first:last])
            wide = weights.astype(f32)
            inner = jnp.sum(grad_weights * wide, axis=-1, keepdims=True)
            grad_scores = (wide * (grad_weights - inner) * SCALE).astype(bf16)
            dq.append(dot_nn(grad_scores, k_ref[frame, :, first:last]))
            dk.append(dot_tn(grad_scores, q_ref[frame, :, first:last]))
            dv.append(dot_tn(weights, grad_head))
        grad_xn = dot_nn(merge_heads(dq).astype(bf16), qkv_ref[:INNER, :])
        grad_xn += dot_nn(merge_heads(dk).astype(bf16), qkv_ref[INNER : 2 * INNER, :])
        grad_xn += dot_nn(merge_heads(dv).astype(bf16), qkv_ref[2 * INNER :, :])
        back = normalize_back(grad_xn, xn_ref[frame].astype(f32), inverse_ref[frame])
        grad_x1 = grad_ref[:, own, :].reshape(patches, width)
        result_ref[frame] = (grad_x1.astype(f32) + back).astype(bf16)
        copy = pltpu.make_async_copy(
            result_ref.at[frame], result_hbm.at[frame], result_sem.at[frame]
        )
        copy.start()
        copies.append(copy)
    for copy in copies:
        copy.wait()


def slot_columns(times_row, count, rows):
    slots = times_row.shape[1]
    valid = jnp.where(times_row < count, 1.0, 0.0).astype(f32)
    row_slot = lax.broadcasted_iota(jnp.int32, (rows, slots), 0) // GROUP
    slot = lax.broadcasted_iota(jnp.int32, (rows, slots), 1)
    column = jnp.sum(jnp.where(row_slot == slot, valid, 0.0), axis=1, keepdims=True)
    return valid, column


def temporal_forward(
    count_ref,
    row_ref,
    x1_ref,
    embed_ref,
    qkv_ref,
    out_ref,
    proj_ref,
    text_ref,
    send_ref,
    tn_ref,
    inverse_ref,
    q_ref,
    k_ref,
    p_ref,
    c_ref,
):
    slots, share, width = x1_ref.shape
    groups = share // GROUP
    rows = slots * GROUP
    count = count_ref[...]
    lookup = jnp.where(
        lax.broadcasted_iota(jnp.int32, (embed_ref.shape[0], slots), 0) == row_ref[...], 1.0, 0.0
    ).astype(bf16)
    added = None
    for part in split_terms(embed_ref[...], 3):
        term = dot_tn(lookup, part)
        added = term if added is None else added + term
    valid, valid_column = slot_columns(row_ref[...], count, rows)
    chunk = 8
    pooled = jnp.zeros((1, width), f32)
    for start in range(0, slots, chunk):
        y = x1_ref[start : start + chunk].astype(f32) + added[start : start + chunk][:, None, :]
        part = jnp.sum(y, axis=1)
        slot_valid = jnp.concatenate(
            [valid_column[(start + i) * GROUP : (start + i) * GROUP + 1] for i in range(chunk)],
            axis=0,
        )
        pooled = pooled + jnp.sum(part * slot_valid, axis=0, keepdims=True)
        normed, inverse = normalize(y)
        for group in range(groups):
            own = slice(group * GROUP, (group + 1) * GROUP)
            at = pl.ds(group * rows + start * GROUP, chunk * GROUP)
            tn_ref[at, :] = normed[:, own, :].reshape(chunk * GROUP, width).astype(bf16)
            inverse_ref[at, :] = inverse[:, own, :].reshape(chunk * GROUP, 1)
    row_index = lax.broadcasted_iota(jnp.int32, (rows, rows), 0)
    column_index = lax.broadcasted_iota(jnp.int32, (rows, rows), 1)
    spread = jnp.where(
        lax.broadcasted_iota(jnp.int32, (slots, rows), 0)
        == lax.broadcasted_iota(jnp.int32, (slots, rows), 1) // GROUP,
        1.0,
        0.0,
    ).astype(bf16)
    key_valid = dot_nn(jnp.broadcast_to(valid, (GROUP, slots)).astype(bf16), spread)[:1]
    allowed = (row_index % GROUP == column_index % GROUP) & (key_valid > 0.5)
    for group in range(groups):
        at = pl.ds(group * rows, rows)
        q_ref[at, :] = dot_nt(tn_ref[at, :], qkv_ref[:INNER, :]).astype(bf16)
        k_ref[at, :] = dot_nt(tn_ref[at, :], qkv_ref[INNER : 2 * INNER, :]).astype(bf16)
        for head in range(HEADS):
            first, last, _ = window(head)
            query = keep_head(q_ref[at, first:last], head)
            scores = dot_nt(query, k_ref[at, first:last]) * SCALE
            raised = jnp.where(allowed, jnp.exp(scores), 0.0)
            weights = raised * (valid_column / jnp.sum(raised, axis=-1, keepdims=True))
            p_ref[group, head] = weights.astype(bf16)
            c_ref[head : head + 1, at] = jnp.sum(weights, axis=0, keepdims=True)
    gathered = exact(dot_nn, c_ref[...], tn_ref[...], 2)
    mixed_all = exact(dot_nt, gathered, qkv_ref[2 * INNER :, :])
    lane = lax.broadcasted_iota(jnp.int32, mixed_all.shape, 1)
    head_row = lax.broadcasted_iota(jnp.int32, mixed_all.shape, 0)
    own_lane = (lane >= head_row * HD) & (lane < head_row * HD + HD)
    mixed = jnp.sum(jnp.where(own_lane, mixed_all, 0.0), axis=0, keepdims=True)
    feature = pooled + exact(dot_nn, jnp.broadcast_to(mixed, (GROUP, INNER)), out_ref[...])[:1]
    z = exact(dot_nn, jnp.broadcast_to(feature, (GROUP, width)), proj_ref[...])[:1]
    z = z / (count.astype(f32) * float(PATCHES))
    embed_size = z.shape[1]
    send_ref[:, :, :embed_size] = jnp.broadcast_to(
        z[None], (send_ref.shape[0], 1, embed_size)
    )
    tiles = embed_size // LANES
    own_tile = lax.axis_index("frame") // (lax.axis_size("frame") // tiles)
    piece = jnp.zeros((1, LANES), f32)
    for tile in range(tiles):
        held = text_ref[:, tile * LANES : (tile + 1) * LANES]
        piece = jnp.where(own_tile == tile, held, piece)
    send_ref[:, :, embed_size:] = jnp.broadcast_to(piece[None], (send_ref.shape[0], 1, LANES))


PATCHES = 256


def unit_rows(matrix):
    inverse = lax.rsqrt(jnp.sum(matrix * matrix, axis=-1, keepdims=True) + EPSILON)
    return matrix * inverse, inverse


def temporal_backward(
    batch,
    cotangent,
    count_ref,
    row_ref,
    parts_ref,
    tn_ref,
    inverse_ref,
    q_ref,
    k_ref,
    p_ref,
    c_ref,
    qkv_ref,
    out_ref,
    proj_ref,
    grad_ref,
    loss_ref,
    dtn_ref,
):
    slots, share, width = grad_ref.shape
    groups = share // GROUP
    rows = slots * GROUP
    count = count_ref[...]
    clips = batch
    per_clip = parts_ref.shape[0] // clips
    embed_size = proj_ref.shape[1]
    parts = parts_ref[:, 0, :].reshape(clips, per_clip, parts_ref.shape[2])
    z = jnp.sum(parts[:, :, :embed_size], axis=1)
    tiles = embed_size // LANES
    text = jnp.concatenate(
        [parts[:, i * (per_clip // tiles), embed_size:] for i in range(tiles)], axis=1
    )
    e, inverse_z = unit_rows(z)
    u, _ = unit_rows(text)
    logits = (
        lax.dot_general(
            e,
            u,
            (((1,), (1,)), ((), ())),
            precision=lax.Precision.HIGHEST,
            preferred_element_type=f32,
        )
        * SHARPNESS
    )
    raised = jnp.exp(logits)
    row_total = jnp.sum(raised, axis=1, keepdims=True)
    column_total = jnp.sum(raised, axis=0, keepdims=True)
    diagonal = lax.broadcasted_iota(jnp.int32, logits.shape, 0) == lax.broadcasted_iota(
        jnp.int32, logits.shape, 1
    )
    loss = (
        0.5 * jnp.sum(jnp.log(row_total), axis=0, keepdims=True)
        + 0.5 * jnp.sum(jnp.log(column_total), axis=1, keepdims=True)
        - jnp.sum(jnp.sum(jnp.where(diagonal, logits, 0.0), axis=1, keepdims=True), axis=0, keepdims=True)
    )
    loss_ref[...] = loss
    shares = 0.5 * (raised / row_total + raised / column_total) - jnp.where(diagonal, 1.0, 0.0)
    grad_e = (cotangent * SHARPNESS) * lax.dot_general(
        shares,
        u,
        (((1,), (0,)), ((), ())),
        precision=lax.Precision.HIGHEST,
        preferred_element_type=f32,
    )
    grad_z = inverse_z * (grad_e - e * jnp.sum(e * grad_e, axis=-1, keepdims=True))
    own = lax.broadcasted_iota(jnp.int32, grad_z.shape, 0) == lax.axis_index("batch")
    grad_own = jnp.sum(jnp.where(own, grad_z, 0.0), axis=0, keepdims=True)
    grad_own = grad_own / (count.astype(f32) * float(PATCHES))
    grad_feature = exact(dot_nt, jnp.broadcast_to(grad_own, grad_z.shape), proj_ref[...])
    grad_mixed = exact(dot_nt, grad_feature, out_ref[...])
    lane = lax.broadcasted_iota(jnp.int32, grad_mixed.shape, 1)
    head_row = lax.broadcasted_iota(jnp.int32, grad_mixed.shape, 0)
    own_lane = (lane >= head_row * HD) & (lane < head_row * HD + HD)
    value_grad = exact(dot_nn, jnp.where(own_lane, grad_mixed, 0.0), qkv_ref[2 * INNER :, :])
    high, low = split_terms(value_grad, 2)
    scores_grad = exact(dot_nt, value_grad, tn_ref[...], 2)
    c_high, c_low = split_terms(c_ref[...], 2)
    _, valid_column = slot_columns(row_ref[...], count, rows)
    for group in range(groups):
        at = pl.ds(group * rows, rows)
        dq, dk = [], []
        for head in range(HEADS):
            first, last, _ = window(head)
            weights = p_ref[group, head].astype(f32)
            along = scores_grad[head : head + 1, group * rows : (group + 1) * rows]
            inner = jnp.sum(weights * along, axis=-1, keepdims=True)
            grad_scores = (weights * (along - inner) * SCALE).astype(bf16)
            dq.append(dot_nn(grad_scores, k_ref[at, first:last]))
            dk.append(dot_tn(grad_scores, q_ref[at, first:last]))
        own = slice(group * rows, (group + 1) * rows)
        weights_c = jnp.concatenate([c_high[:, own], c_high[:, own], c_low[:, own]], axis=0)
        value_rows = jnp.concatenate([high, low, high], axis=0)
        grad_tn = dot_nn(merge_heads(dq).astype(bf16), qkv_ref[:INNER, :])
        grad_tn += dot_nn(merge_heads(dk).astype(bf16), qkv_ref[INNER : 2 * INNER, :])
        dtn_ref[at, :] = grad_tn + dot_tn(weights_c, value_rows)
    chunk = 8
    for start in range(0, slots, chunk):
        pieces = []
        for group in range(groups):
            at = pl.ds(group * rows + start * GROUP, chunk * GROUP)
            back = normalize_back(dtn_ref[at, :], tn_ref[at, :].astype(f32), inverse_ref[at, :])
            back = (
                back
                + valid_column[start * GROUP : (start + chunk) * GROUP] * grad_feature[:1]
            )
            pieces.append(back.reshape(chunk, 1, GROUP, width))
        joined = jnp.concatenate(pieces, axis=1).reshape(chunk, share, width)
        grad_ref[start : start + chunk] = joined.astype(bf16)


def cost(microseconds):
    return pl.CostEstimate(flops=microseconds * 10**9, bytes_accessed=0, transcendentals=0)


def per_device(
    tokens,
    frame_time,
    valid_count,
    spatial_qkv,
    spatial_out,
    temporal_qkv,
    temporal_out,
    time_embed,
    video_proj,
    text_embed,
):
    frames_in = tokens[0]
    local_frames, patches, width = frames_in.shape
    owners = lax.axis_size("frame")
    clips = lax.axis_size("batch")
    devices = owners * clips
    share = patches // owners
    slots = owners * local_frames
    groups = share // GROUP
    rows = slots * share
    shape = jax.ShapeDtypeStruct
    traded = (owners, local_frames * share, width)
    params = pltpu.CompilerParams(vmem_limit_bytes=20 * MIB)
    spatial_qkv = spatial_qkv.T
    temporal_qkv = temporal_qkv.T
    counts = valid_count.reshape(1, 1)

    xn, xn_inverse, counts = pl.pallas_call(
        spatial_norm,
        out_shape=(
            shape(frames_in.shape, bf16),
            shape((local_frames, patches, 1), f32),
            shape((1, 1), jnp.int32),
        ),
        in_specs=[VMEM] * 2,
        out_specs=(VMEM,) * 3,
        compiler_params=params,
        cost_estimate=cost(1),
        name="spatial_norm",
    )(counts, frames_in)
    x1, q, k, v, p = pl.pallas_call(
        spatial_forward,
        out_shape=(
            shape(traded, bf16),
            shape((local_frames, patches, INNER), bf16),
            shape((local_frames, patches, INNER), bf16),
            shape((local_frames, patches, INNER), bf16),
            shape((local_frames, HEADS, patches, patches), bf16),
        ),
        in_specs=[VMEM] * 4,
        out_specs=(VMEM,) * 5,
        compiler_params=params,
        cost_estimate=cost(8),
        name="spatial_forward",
    )(frames_in, xn, spatial_qkv, spatial_out)

    x1 = lax.all_to_all(x1, "frame", split_axis=0, concat_axis=0, tiled=True)
    x1 = x1.reshape(slots, share, width)
    embed_size = text_embed.shape[1]
    send, tn, inverse, tq, tk, tp, c = pl.pallas_call(
        temporal_forward,
        out_shape=(
            shape((devices, 1, embed_size + LANES), f32),
            shape((rows, width), bf16),
            shape((rows, 1), f32),
            shape((rows, INNER), bf16),
            shape((rows, INNER), bf16),
            shape((groups, HEADS, slots * GROUP, slots * GROUP), bf16),
            shape((HEADS, rows), f32),
        ),
        in_specs=[VMEM] * 8,
        out_specs=(VMEM,) * 7,
        compiler_params=params,
        cost_estimate=cost(7),
        name="temporal_forward",
    )(
        counts,
        frame_time,
        x1,
        time_embed,
        temporal_qkv,
        temporal_out,
        video_proj,
        text_embed,
    )

    parts = lax.all_to_all(send, ("batch", "frame"), split_axis=0, concat_axis=0, tiled=True)
    grad_x1, loss = pl.pallas_call(
        functools.partial(temporal_backward, clips, float(slots * patches)),
        out_shape=(shape((slots, share, width), bf16), shape((1, 1), f32)),
        in_specs=[VMEM] * 12,
        out_specs=(VMEM,) * 2,
        scratch_shapes=[pltpu.VMEM((rows, width), f32)],
        compiler_params=params,
        cost_estimate=cost(8),
        name="temporal_backward",
    )(
        counts,
        frame_time,
        parts,
        tn,
        inverse,
        tq,
        tk,
        tp,
        c,
        temporal_qkv,
        temporal_out,
        video_proj,
    )
    grad_x1 = lax.all_to_all(
        grad_x1.reshape(traded), "frame", split_axis=0, concat_axis=0, tiled=True
    )
    result = pl.pallas_call(
        spatial_backward,
        out_shape=shape(frames_in.shape, bf16),
        in_specs=[VMEM] * 9,
        out_specs=HBM,
        scratch_shapes=[
            pltpu.VMEM(frames_in.shape, bf16),
            pltpu.SemaphoreType.DMA((local_frames,)),
        ],
        compiler_params=params,
        cost_estimate=cost(12),
        name="spatial_backward",
    )(grad_x1, xn, xn_inverse, spatial_qkv, spatial_out, q, k, v, p)
    return (result[None], loss[0, 0])


def solution(mesh):
    placed = (
        P("batch", "frame", None, None),
        P("batch", None),
        P("batch"),
        P(),
        P(),
        P(),
        P(),
        P(),
        P(),
        P("batch", None),
    )
    return jax.shard_map(
        per_device,
        mesh=mesh,
        in_specs=placed,
        out_specs=(P("batch", "frame", None, None), P()),
        check_vma=False,
    )
```

```python
import functools
import math

import jax
import jax.numpy as jnp
from jax import lax
from jax.experimental import pallas as pl
from jax.experimental.pallas import tpu as pltpu
from jax.sharding import PartitionSpec as P

HEADS = 8
HD = 88
INNER = HEADS * HD
LANES = 128
GROUP = 8
EPSILON = 1e-06
SHARPNESS = 1.0 / 0.07
SCALE = 1.0 / math.sqrt(HD)
QUERY_SCALE = SCALE / math.log(2.0)
KEY_BACK = math.log(2.0)
MIB = 1024 * 1024

bf16 = jnp.bfloat16
f32 = jnp.float32
VMEM = pl.BlockSpec(memory_space=pltpu.VMEM)
HBM = pl.BlockSpec(memory_space=pltpu.HBM)


def dot_nn(left, right):
    return lax.dot_general(left, right, (((1,), (0,)), ((), ())), preferred_element_type=f32)


def dot_nt(left, right):
    return lax.dot_general(left, right, (((1,), (1,)), ((), ())), preferred_element_type=f32)


def dot_tn(left, right):
    return lax.dot_general(left, right, (((0,), (0,)), ((), ())), preferred_element_type=f32)


def split_terms(values, terms):
    parts = []
    rest = values
    for _ in range(terms):
        part = rest.astype(bf16)
        parts.append(part)
        rest = rest - part.astype(f32)
    return parts


def exact(dot, values, matrix, terms=3):
    rows = values.shape[0]
    products = dot(jnp.concatenate(split_terms(values, terms), axis=0), matrix)
    total = products[:rows]
    for term in range(1, terms):
        total = total + products[term * rows : (term + 1) * rows]
    return total


def window(head):
    first = head * HD // LANES * LANES
    last = min(-(-(head + 1) * HD // LANES) * LANES, INNER)
    return first, last, head * HD - first


def head_lanes(rows, head):
    first, last, offset = window(head)
    lane = lax.broadcasted_iota(jnp.int32, (rows, last - first), 1)
    return (lane >= offset) & (lane < offset + HD)


def keep_head(values, head):
    return jnp.where(head_lanes(values.shape[0], head), values, jnp.zeros_like(values))


def merge_heads(products):
    tiles = []
    for start in range(0, INNER, LANES):
        width = min(LANES, INNER - start)
        tile = None
        for head in range(HEADS):
            first, last, offset = window(head)
            if first <= start < last:
                piece = products[head][:, start - first : start - first + width]
                if tile is None:
                    tile = piece
                else:
                    lane = lax.broadcasted_iota(jnp.int32, piece.shape, 1)
                    tile = jnp.where(lane >= head * HD - start, piece, tile)
        tiles.append(tile)
    return jnp.concatenate(tiles, axis=1)


def normalize(values):
    center = values - jnp.mean(values, axis=-1, keepdims=True)
    spread = jnp.mean(center * center, axis=-1, keepdims=True)
    inverse = lax.rsqrt(spread + EPSILON)
    return center * inverse, inverse


def normalize_back(grad, normed, inverse):
    return inverse * (
        grad
        - jnp.mean(grad, axis=-1, keepdims=True)
        - normed * jnp.mean(grad * normed, axis=-1, keepdims=True)
    )


def spatial_norm(count_ref, tok_ref, xn_ref, inverse_ref, count_out_ref):
    count_out_ref[...] = count_ref[...]
    for frame in range(tok_ref.shape[0]):
        normed, inverse = normalize(tok_ref[frame].astype(f32))
        xn_ref[frame] = normed.astype(bf16)
        inverse_ref[frame] = inverse


def spatial_forward(
    tok_ref, xn_ref, qkv_ref, out_ref, x1_ref, q_ref, k_ref, v_ref, p_ref, so_ref
):
    frames, patches, _ = tok_ref.shape
    owners = x1_ref.shape[0]
    share = patches // owners
    for frame in range(frames):
        packed = dot_nt(xn_ref[frame], qkv_ref[...])
        q_ref[frame] = (packed[:, :INNER] * QUERY_SCALE).astype(bf16)
        k_ref[frame] = packed[:, INNER : 2 * INNER].astype(bf16)
        v_ref[frame] = packed[:, 2 * INNER :].astype(bf16)
        scores = []
        for head in range(HEADS):
            first, last, _ = window(head)
            query = keep_head(q_ref[frame, :, first:last], head)
            scores.append(dot_nt(query, k_ref[frame, :, first:last]))
        for head in range(HEADS):
            raised = jnp.exp2(scores[head])
            weights = raised * (1.0 / jnp.sum(raised, axis=-1, keepdims=True))
            p_ref[frame, head] = weights.astype(bf16)
        mixed = []
        for head in range(HEADS):
            first, last, _ = window(head)
            mixed.append(dot_nn(p_ref[frame, head], v_ref[frame, :, first:last]))
        so_ref[frame] = merge_heads(mixed).astype(bf16)
        update = dot_nn(so_ref[frame], out_ref[...])
        x1 = (tok_ref[frame].astype(f32) + update).astype(bf16)
        own = slice(frame * share, (frame + 1) * share)
        x1_ref[:, own, :] = x1.reshape(owners, share, x1.shape[-1])


def spatial_backward(
    grad_ref,
    xn_ref,
    inverse_ref,
    qkv_ref,
    out_ref,
    q_ref,
    k_ref,
    v_ref,
    p_ref,
    so_ref,
    result_hbm,
    result_ref,
    result_sem,
):
    frames, patches, width = xn_ref.shape
    owners = grad_ref.shape[0]
    share = patches // owners
    copies = []
    for frame in range(frames):
        own = slice(frame * share, (frame + 1) * share)
        grad_x1 = grad_ref[:, own, :].reshape(patches, width)
        grad_so = dot_nt(grad_x1, out_ref[...]).astype(bf16)
        dv = []
        for head in range(HEADS):
            first, last, _ = window(head)
            dv.append(dot_tn(p_ref[frame, head], grad_so[:, first:last]))
        dv = merge_heads(dv).astype(bf16)
        grad_weights, inner = [], []
        for head in range(HEADS):
            first, last, _ = window(head)
            grad_head = keep_head(grad_so[:, first:last], head)
            along = grad_head.astype(f32) * so_ref[frame, :, first:last].astype(f32)
            inner.append(jnp.sum(along, axis=-1, keepdims=True))
            grad_weights.append(dot_nt(grad_head, v_ref[frame, :, first:last]))
        dq, dk = [], []
        for head in range(HEADS):
            first, last, _ = window(head)
            weights = p_ref[frame, head].astype(f32)
            grad_scores = (weights * (grad_weights[head] - inner[head])).astype(bf16)
            dq.append(dot_nn(grad_scores, k_ref[frame, :, first:last]))
            dk.append(dot_tn(grad_scores, q_ref[frame, :, first:last]))
        grad_xn = dot_nn((merge_heads(dq) * SCALE).astype(bf16), qkv_ref[:INNER, :])
        grad_xn += dot_nn((merge_heads(dk) * KEY_BACK).astype(bf16), qkv_ref[INNER : 2 * INNER, :])
        grad_xn += dot_nn(dv, qkv_ref[2 * INNER :, :])
        back = normalize_back(grad_xn, xn_ref[frame].astype(f32), inverse_ref[frame])
        grad_x1 = grad_ref[:, own, :].reshape(patches, width)
        result_ref[frame] = (grad_x1.astype(f32) + back).astype(bf16)
        copy = pltpu.make_async_copy(
            result_ref.at[frame], result_hbm.at[frame], result_sem.at[frame]
        )
        copy.start()
        copies.append(copy)
    for copy in copies:
        copy.wait()


def slot_columns(times_row, count, rows):
    slots = times_row.shape[1]
    valid = jnp.where(times_row < count, 1.0, 0.0).astype(f32)
    row_slot = lax.broadcasted_iota(jnp.int32, (rows, slots), 0) // GROUP
    slot = lax.broadcasted_iota(jnp.int32, (rows, slots), 1)
    column = jnp.sum(jnp.where(row_slot == slot, valid, 0.0), axis=1, keepdims=True)
    return valid, column


def temporal_forward(
    count_ref,
    row_ref,
    x1_ref,
    embed_ref,
    qkv_ref,
    out_ref,
    proj_ref,
    text_ref,
    send_ref,
    tn_ref,
    inverse_ref,
    q_ref,
    k_ref,
    p_ref,
    c_ref,
):
    slots, share, width = x1_ref.shape
    groups = share // GROUP
    rows = slots * GROUP
    count = count_ref[...]
    lookup = jnp.where(
        lax.broadcasted_iota(jnp.int32, (embed_ref.shape[0], slots), 0) == row_ref[...], 1.0, 0.0
    ).astype(bf16)
    added = None
    for part in split_terms(embed_ref[...], 3):
        term = dot_tn(lookup, part)
        added = term if added is None else added + term
    valid, valid_column = slot_columns(row_ref[...], count, rows)
    chunk = 8
    pooled = jnp.zeros((1, width), f32)
    for start in range(0, slots, chunk):
        y = x1_ref[start : start + chunk].astype(f32) + added[start : start + chunk][:, None, :]
        part = jnp.sum(y, axis=1)
        slot_valid = jnp.concatenate(
            [valid_column[(start + i) * GROUP : (start + i) * GROUP + 1] for i in range(chunk)],
            axis=0,
        )
        pooled = pooled + jnp.sum(part * slot_valid, axis=0, keepdims=True)
        normed, inverse = normalize(y)
        for group in range(groups):
            own = slice(group * GROUP, (group + 1) * GROUP)
            at = pl.ds(group * rows + start * GROUP, chunk * GROUP)
            tn_ref[at, :] = normed[:, own, :].reshape(chunk * GROUP, width).astype(bf16)
            inverse_ref[at, :] = inverse[:, own, :].reshape(chunk * GROUP, 1)
    row_index = lax.broadcasted_iota(jnp.int32, (rows, rows), 0)
    column_index = lax.broadcasted_iota(jnp.int32, (rows, rows), 1)
    spread = jnp.where(
        lax.broadcasted_iota(jnp.int32, (slots, rows), 0)
        == lax.broadcasted_iota(jnp.int32, (slots, rows), 1) // GROUP,
        1.0,
        0.0,
    ).astype(bf16)
    key_valid = dot_nn(jnp.broadcast_to(valid, (GROUP, slots)).astype(bf16), spread)[:1]
    allowed = (row_index % GROUP == column_index % GROUP) & (key_valid > 0.5)
    for group in range(groups):
        at = pl.ds(group * rows, rows)
        packed = dot_nt(tn_ref[at, :], qkv_ref[: 2 * INNER, :])
        q_ref[at, :] = (packed[:, :INNER] * QUERY_SCALE).astype(bf16)
        k_ref[at, :] = packed[:, INNER:].astype(bf16)
        scores = []
        for head in range(HEADS):
            first, last, _ = window(head)
            query = keep_head(q_ref[at, first:last], head)
            scores.append(dot_nt(query, k_ref[at, first:last]))
        for head in range(HEADS):
            raised = jnp.where(allowed, jnp.exp2(scores[head]), 0.0)
            weights = raised * (valid_column / jnp.sum(raised, axis=-1, keepdims=True))
            p_ref[group, head] = weights.astype(bf16)
            c_ref[head : head + 1, at] = jnp.sum(weights, axis=0, keepdims=True)
    gathered = exact(dot_nn, c_ref[...], tn_ref[...], 2)
    mixed_all = exact(dot_nt, gathered, qkv_ref[2 * INNER :, :])
    lane = lax.broadcasted_iota(jnp.int32, mixed_all.shape, 1)
    head_row = lax.broadcasted_iota(jnp.int32, mixed_all.shape, 0)
    own_lane = (lane >= head_row * HD) & (lane < head_row * HD + HD)
    mixed = jnp.sum(jnp.where(own_lane, mixed_all, 0.0), axis=0, keepdims=True)
    feature = pooled + exact(dot_nn, jnp.broadcast_to(mixed, (GROUP, INNER)), out_ref[...])[:1]
    z = exact(dot_nn, jnp.broadcast_to(feature, (GROUP, width)), proj_ref[...])[:1]
    z = z / (count.astype(f32) * float(PATCHES))
    embed_size = z.shape[1]
    send_ref[:, :, :embed_size] = jnp.broadcast_to(
        z[None], (send_ref.shape[0], 1, embed_size)
    )
    tiles = embed_size // LANES
    own_tile = lax.axis_index("frame") // (lax.axis_size("frame") // tiles)
    piece = jnp.zeros((1, LANES), f32)
    for tile in range(tiles):
        held = text_ref[:, tile * LANES : (tile + 1) * LANES]
        piece = jnp.where(own_tile == tile, held, piece)
    send_ref[:, :, embed_size:] = jnp.broadcast_to(piece[None], (send_ref.shape[0], 1, LANES))


PATCHES = 256


def unit_rows(matrix):
    inverse = lax.rsqrt(jnp.sum(matrix * matrix, axis=-1, keepdims=True) + EPSILON)
    return matrix * inverse, inverse


def temporal_backward(
    batch,
    cotangent,
    count_ref,
    row_ref,
    parts_ref,
    tn_ref,
    inverse_ref,
    q_ref,
    k_ref,
    p_ref,
    c_ref,
    qkv_ref,
    out_ref,
    proj_ref,
    grad_ref,
    loss_ref,
    dtn_ref,
):
    slots, share, width = grad_ref.shape
    groups = share // GROUP
    rows = slots * GROUP
    count = count_ref[...]
    clips = batch
    per_clip = parts_ref.shape[0] // clips
    embed_size = proj_ref.shape[1]
    parts = parts_ref[:, 0, :].reshape(clips, per_clip, parts_ref.shape[2])
    z = jnp.sum(parts[:, :, :embed_size], axis=1)
    tiles = embed_size // LANES
    text = jnp.concatenate(
        [parts[:, i * (per_clip // tiles), embed_size:] for i in range(tiles)], axis=1
    )
    e, inverse_z = unit_rows(z)
    u, _ = unit_rows(text)
    logits = (
        lax.dot_general(
            e,
            u,
            (((1,), (1,)), ((), ())),
            precision=lax.Precision.HIGHEST,
            preferred_element_type=f32,
        )
        * SHARPNESS
    )
    raised = jnp.exp(logits)
    row_total = jnp.sum(raised, axis=1, keepdims=True)
    column_total = jnp.sum(raised, axis=0, keepdims=True)
    diagonal = lax.broadcasted_iota(jnp.int32, logits.shape, 0) == lax.broadcasted_iota(
        jnp.int32, logits.shape, 1
    )
    loss = (
        0.5 * jnp.sum(jnp.log(row_total), axis=0, keepdims=True)
        + 0.5 * jnp.sum(jnp.log(column_total), axis=1, keepdims=True)
        - jnp.sum(jnp.sum(jnp.where(diagonal, logits, 0.0), axis=1, keepdims=True), axis=0, keepdims=True)
    )
    loss_ref[...] = loss
    shares = 0.5 * (raised / row_total + raised / column_total) - jnp.where(diagonal, 1.0, 0.0)
    grad_e = (cotangent * SHARPNESS) * lax.dot_general(
        shares,
        u,
        (((1,), (0,)), ((), ())),
        precision=lax.Precision.HIGHEST,
        preferred_element_type=f32,
    )
    grad_z = inverse_z * (grad_e - e * jnp.sum(e * grad_e, axis=-1, keepdims=True))
    own = lax.broadcasted_iota(jnp.int32, grad_z.shape, 0) == lax.axis_index("batch")
    grad_own = jnp.sum(jnp.where(own, grad_z, 0.0), axis=0, keepdims=True)
    grad_own = grad_own / (count.astype(f32) * float(PATCHES))
    grad_feature = exact(dot_nt, jnp.broadcast_to(grad_own, grad_z.shape), proj_ref[...])
    grad_mixed = exact(dot_nt, grad_feature, out_ref[...])
    lane = lax.broadcasted_iota(jnp.int32, grad_mixed.shape, 1)
    head_row = lax.broadcasted_iota(jnp.int32, grad_mixed.shape, 0)
    own_lane = (lane >= head_row * HD) & (lane < head_row * HD + HD)
    value_grad = exact(dot_nn, jnp.where(own_lane, grad_mixed, 0.0), qkv_ref[2 * INNER :, :])
    high, low = split_terms(value_grad, 2)
    scores_grad = exact(dot_nt, value_grad, tn_ref[...], 2)
    c_high, c_low = split_terms(c_ref[...], 2)
    _, valid_column = slot_columns(row_ref[...], count, rows)
    for group in range(groups):
        at = pl.ds(group * rows, rows)
        grad_scores = []
        for head in range(HEADS):
            weights = p_ref[group, head].astype(f32)
            along = scores_grad[head : head + 1, group * rows : (group + 1) * rows]
            inner = jnp.sum(weights * along, axis=-1, keepdims=True)
            grad_scores.append((weights * (along - inner)).astype(bf16))
        dq, dk = [], []
        for head in range(HEADS):
            first, last, _ = window(head)
            dq.append(dot_nn(grad_scores[head], k_ref[at, first:last]))
        for head in range(HEADS):
            first, last, _ = window(head)
            dk.append(dot_tn(grad_scores[head], q_ref[at, first:last]))
        own = slice(group * rows, (group + 1) * rows)
        weights_c = jnp.concatenate([c_high[:, own], c_high[:, own], c_low[:, own]], axis=0)
        value_rows = jnp.concatenate([high, low, high], axis=0)
        grad_tn = dot_nn((merge_heads(dq) * SCALE).astype(bf16), qkv_ref[:INNER, :])
        grad_tn += dot_nn((merge_heads(dk) * KEY_BACK).astype(bf16), qkv_ref[INNER : 2 * INNER, :])
        dtn_ref[at, :] = grad_tn + dot_tn(weights_c, value_rows)
    chunk = 8
    for start in range(0, slots, chunk):
        pieces = []
        for group in range(groups):
            at = pl.ds(group * rows + start * GROUP, chunk * GROUP)
            back = normalize_back(dtn_ref[at, :], tn_ref[at, :].astype(f32), inverse_ref[at, :])
            back = (
                back
                + valid_column[start * GROUP : (start + chunk) * GROUP] * grad_feature[:1]
            )
            pieces.append(back.reshape(chunk, 1, GROUP, width))
        joined = jnp.concatenate(pieces, axis=1).reshape(chunk, share, width)
        grad_ref[start : start + chunk] = joined.astype(bf16)


def cost(microseconds):
    return pl.CostEstimate(flops=microseconds * 10**9, bytes_accessed=0, transcendentals=0)


def per_device(
    tokens,
    frame_time,
    valid_count,
    spatial_qkv,
    spatial_out,
    temporal_qkv,
    temporal_out,
    time_embed,
    video_proj,
    text_embed,
):
    frames_in = tokens[0]
    local_frames, patches, width = frames_in.shape
    owners = lax.axis_size("frame")
    clips = lax.axis_size("batch")
    devices = owners * clips
    share = patches // owners
    slots = owners * local_frames
    groups = share // GROUP
    rows = slots * share
    shape = jax.ShapeDtypeStruct
    traded = (owners, local_frames * share, width)
    params = pltpu.CompilerParams(vmem_limit_bytes=20 * MIB)
    spatial_qkv = spatial_qkv.T
    temporal_qkv = temporal_qkv.T
    counts = valid_count.reshape(1, 1)

    xn, xn_inverse, counts = pl.pallas_call(
        spatial_norm,
        out_shape=(
            shape(frames_in.shape, bf16),
            shape((local_frames, patches, 1), f32),
            shape((1, 1), jnp.int32),
        ),
        in_specs=[VMEM] * 2,
        out_specs=(VMEM,) * 3,
        compiler_params=params,
        cost_estimate=cost(30),
        name="spatial_norm",
    )(counts, frames_in)
    x1, q, k, v, p, so = pl.pallas_call(
        spatial_forward,
        out_shape=(
            shape(traded, bf16),
            shape((local_frames, patches, INNER), bf16),
            shape((local_frames, patches, INNER), bf16),
            shape((local_frames, patches, INNER), bf16),
            shape((local_frames, HEADS, patches, patches), bf16),
            shape((local_frames, patches, INNER), bf16),
        ),
        in_specs=[VMEM] * 4,
        out_specs=(VMEM,) * 6,
        compiler_params=params,
        cost_estimate=cost(8),
        name="spatial_forward",
    )(frames_in, xn, spatial_qkv, spatial_out)

    x1 = lax.all_to_all(x1, "frame", split_axis=0, concat_axis=0, tiled=True)
    x1 = x1.reshape(slots, share, width)
    embed_size = text_embed.shape[1]
    send, tn, inverse, tq, tk, tp, c = pl.pallas_call(
        temporal_forward,
        out_shape=(
            shape((devices, 1, embed_size + LANES), f32),
            shape((rows, width), bf16),
            shape((rows, 1), f32),
            shape((rows, INNER), bf16),
            shape((rows, INNER), bf16),
            shape((groups, HEADS, slots * GROUP, slots * GROUP), bf16),
            shape((HEADS, rows), f32),
        ),
        in_specs=[VMEM] * 8,
        out_specs=(VMEM,) * 7,
        compiler_params=params,
        cost_estimate=cost(7),
        name="temporal_forward",
    )(
        counts,
        frame_time,
        x1,
        time_embed,
        temporal_qkv,
        temporal_out,
        video_proj,
        text_embed,
    )

    parts = lax.all_to_all(send, ("batch", "frame"), split_axis=0, concat_axis=0, tiled=True)
    grad_x1, loss = pl.pallas_call(
        functools.partial(temporal_backward, clips, float(slots * patches)),
        out_shape=(shape((slots, share, width), bf16), shape((1, 1), f32)),
        in_specs=[VMEM] * 12,
        out_specs=(VMEM,) * 2,
        scratch_shapes=[pltpu.VMEM((rows, width), f32)],
        compiler_params=params,
        cost_estimate=cost(8),
        name="temporal_backward",
    )(
        counts,
        frame_time,
        parts,
        tn,
        inverse,
        tq,
        tk,
        tp,
        c,
        temporal_qkv,
        temporal_out,
        video_proj,
    )
    grad_x1 = lax.all_to_all(
        grad_x1.reshape(traded), "frame", split_axis=0, concat_axis=0, tiled=True
    )
    result = pl.pallas_call(
        spatial_backward,
        out_shape=shape(frames_in.shape, bf16),
        in_specs=[VMEM] * 10,
        out_specs=HBM,
        scratch_shapes=[
            pltpu.VMEM(frames_in.shape, bf16),
            pltpu.SemaphoreType.DMA((local_frames,)),
        ],
        compiler_params=params,
        cost_estimate=cost(12),
        name="spatial_backward",
    )(grad_x1, xn, xn_inverse, spatial_qkv, spatial_out, q, k, v, p, so)
    return (result[None], loss[0, 0])


def solution(mesh):
    placed = (
        P("batch", "frame", None, None),
        P("batch", None),
        P("batch"),
        P(),
        P(),
        P(),
        P(),
        P(),
        P(),
        P("batch", None),
    )
    return jax.shard_map(
        per_device,
        mesh=mesh,
        in_specs=placed,
        out_specs=(P("batch", "frame", None, None), P()),
        check_vma=False,
    )
```

```python
import functools
import math

import jax
import jax.numpy as jnp
from jax import lax
from jax.experimental import pallas as pl
from jax.experimental.pallas import tpu as pltpu
from jax.sharding import PartitionSpec as P

HEADS = 8
HD = 88
INNER = HEADS * HD
LANES = 128
GROUP = 8
PIECES = 4
EPSILON = 1e-06
SHARPNESS = 1.0 / 0.07
SCALE = 1.0 / math.sqrt(HD)
QUERY_SCALE = SCALE / math.log(2.0)
KEY_BACK = math.log(2.0)
MIB = 1024 * 1024

bf16 = jnp.bfloat16
f32 = jnp.float32
VMEM = pl.BlockSpec(memory_space=pltpu.VMEM)
HBM = pl.BlockSpec(memory_space=pltpu.HBM)


def dot_nn(left, right):
    return lax.dot_general(left, right, (((1,), (0,)), ((), ())), preferred_element_type=f32)


def dot_nt(left, right):
    return lax.dot_general(left, right, (((1,), (1,)), ((), ())), preferred_element_type=f32)


def dot_tn(left, right):
    return lax.dot_general(left, right, (((0,), (0,)), ((), ())), preferred_element_type=f32)


def split_terms(values, terms):
    parts = []
    rest = values
    for _ in range(terms):
        part = rest.astype(bf16)
        parts.append(part)
        rest = rest - part.astype(f32)
    return parts


def exact(dot, values, matrix, terms=2):
    rows = values.shape[0]
    products = dot(jnp.concatenate(split_terms(values, terms), axis=0), matrix)
    total = products[:rows]
    for term in range(1, terms):
        total = total + products[term * rows : (term + 1) * rows]
    return total


def window(head):
    first = head * HD // LANES * LANES
    last = min(-(-(head + 1) * HD // LANES) * LANES, INNER)
    return first, last, head * HD - first


def head_lanes(rows, head):
    first, last, offset = window(head)
    lane = lax.broadcasted_iota(jnp.int32, (rows, last - first), 1)
    return (lane >= offset) & (lane < offset + HD)


def keep_head(values, head):
    return jnp.where(head_lanes(values.shape[0], head), values, jnp.zeros_like(values))


def merge_heads(products):
    tiles = []
    for start in range(0, INNER, LANES):
        width = min(LANES, INNER - start)
        tile = None
        for head in range(HEADS):
            first, last, offset = window(head)
            if first <= start < last:
                piece = products[head][:, start - first : start - first + width]
                if tile is None:
                    tile = piece
                else:
                    lane = lax.broadcasted_iota(jnp.int32, piece.shape, 1)
                    tile = jnp.where(lane >= head * HD - start, piece, tile)
        tiles.append(tile)
    return jnp.concatenate(tiles, axis=1)


def normalize(values):
    center = values - jnp.mean(values, axis=-1, keepdims=True)
    spread = jnp.mean(center * center, axis=-1, keepdims=True)
    inverse = lax.rsqrt(spread + EPSILON)
    return center * inverse, inverse


def normalize_back(grad, normed, inverse):
    return inverse * (
        grad
        - jnp.mean(grad, axis=-1, keepdims=True)
        - normed * jnp.mean(grad * normed, axis=-1, keepdims=True)
    )


def spatial_norm(count_ref, tok_ref, xn_ref, inverse_ref, info_ref):
    count = count_ref[...].astype(f32)
    info_ref[0:1, :] = jnp.broadcast_to(count, (1, info_ref.shape[1]))
    scale = 1.0 / (count * float(tok_ref.shape[1]))
    info_ref[1:2, :] = jnp.broadcast_to(scale, (1, info_ref.shape[1]))
    for frame in range(tok_ref.shape[0]):
        normed, inverse = normalize(tok_ref[frame].astype(f32))
        xn_ref[frame] = normed.astype(bf16)
        inverse_ref[frame] = inverse


def spatial_attention(xn_ref, qkv_ref, q_ref, k_ref, v_ref, p_ref, so_ref):
    for frame in range(xn_ref.shape[0]):
        packed = dot_nt(xn_ref[frame], qkv_ref[...])
        q_ref[frame] = (packed[:, :INNER] * QUERY_SCALE).astype(bf16)
        k_ref[frame] = packed[:, INNER : 2 * INNER].astype(bf16)
        v_ref[frame] = packed[:, 2 * INNER :].astype(bf16)
        scores = []
        for head in range(HEADS):
            first, last, _ = window(head)
            query = keep_head(q_ref[frame, :, first:last], head)
            scores.append(dot_nt(query, k_ref[frame, :, first:last]))
        for head in range(HEADS):
            raised = jnp.exp2(scores[head])
            weights = raised * (1.0 / jnp.sum(raised, axis=-1, keepdims=True))
            p_ref[frame, head] = weights.astype(bf16)
        mixed = []
        for head in range(HEADS):
            first, last, _ = window(head)
            mixed.append(dot_nn(p_ref[frame, head], v_ref[frame, :, first:last]))
        so_ref[frame] = merge_heads(mixed).astype(bf16)


def spatial_output(tok_ref, so_ref, out_ref, x1_ref):
    frames, patches, width = tok_ref.shape
    owners = x1_ref.shape[0]
    share = patches // owners
    for frame in range(frames):
        update = dot_nn(so_ref[frame], out_ref[...])
        x1 = (tok_ref[frame].astype(f32) + update).astype(bf16)
        own = slice(frame * share, (frame + 1) * share)
        x1_ref[:, own, :] = x1.reshape(owners, share, width)


def spatial_backward(
    grad_ref,
    xn_ref,
    inverse_ref,
    qkv_ref,
    out_ref,
    q_ref,
    k_ref,
    v_ref,
    p_ref,
    so_ref,
    loss_ref,
    result_hbm,
    loss_hbm,
    result_ref,
    loss_held_ref,
    result_sem,
    loss_sem,
):
    loss_held_ref[...] = loss_ref[:1, :1]
    loss_copy = pltpu.make_async_copy(loss_held_ref, loss_hbm, loss_sem)
    loss_copy.start()
    frames, patches, width = xn_ref.shape
    owners = grad_ref.shape[0]
    share = patches // owners
    copies = []
    for frame in range(frames):
        own = slice(frame * share, (frame + 1) * share)
        grad_x1 = grad_ref[:, own, :].reshape(patches, width)
        grad_so = dot_nt(grad_x1, out_ref[...]).astype(bf16)
        dv = []
        for head in range(HEADS):
            first, last, _ = window(head)
            dv.append(dot_tn(p_ref[frame, head], grad_so[:, first:last]))
        dv = merge_heads(dv).astype(bf16)
        grad_weights, inner = [], []
        for head in range(HEADS):
            first, last, _ = window(head)
            grad_head = keep_head(grad_so[:, first:last], head)
            along = grad_head.astype(f32) * so_ref[frame, :, first:last].astype(f32)
            inner.append(jnp.sum(along, axis=-1, keepdims=True))
            grad_weights.append(dot_nt(grad_head, v_ref[frame, :, first:last]))
        dq, dk = [], []
        for head in range(HEADS):
            first, last, _ = window(head)
            weights = p_ref[frame, head].astype(f32)
            grad_scores = (weights * (grad_weights[head] - inner[head])).astype(bf16)
            dq.append(dot_nn(grad_scores, k_ref[frame, :, first:last]))
            dk.append(dot_tn(grad_scores, q_ref[frame, :, first:last]))
        grad_xn = dot_nn((merge_heads(dq) * SCALE).astype(bf16), qkv_ref[:INNER, :])
        grad_xn += dot_nn((merge_heads(dk) * KEY_BACK).astype(bf16), qkv_ref[INNER : 2 * INNER, :])
        grad_xn += dot_nn(dv, qkv_ref[2 * INNER :, :])
        for piece in range(PIECES):
            size = patches // PIECES
            at = slice(piece * size, (piece + 1) * size)
            back = normalize_back(
                grad_xn[at], xn_ref[frame, at].astype(f32), inverse_ref[frame, at]
            )
            held = slice(piece * owners // PIECES, (piece + 1) * owners // PIECES)
            grad_x1 = grad_ref[held, own, :].reshape(size, width)
            result_ref[frame, at] = (grad_x1.astype(f32) + back).astype(bf16)
            rows = pl.ds(piece * size, size)
            copy = pltpu.make_async_copy(
                result_ref.at[frame, rows],
                result_hbm.at[frame, rows],
                result_sem.at[frame, piece],
            )
            copy.start()
            copies.append(copy)
    for copy in copies + [loss_copy]:
        copy.wait()


def slot_columns(valid, rows):
    slots = valid.shape[1]
    row_slot = lax.broadcasted_iota(jnp.int32, (rows, slots), 0) // GROUP
    slot = lax.broadcasted_iota(jnp.int32, (rows, slots), 1)
    column = jnp.sum(jnp.where(row_slot == slot, valid, 0.0), axis=1, keepdims=True)
    return column


def temporal_forward(
    info_ref,
    times_ref,
    x1_ref,
    embed_ref,
    qkv_ref,
    out_ref,
    proj_ref,
    text_ref,
    send_ref,
    tn_ref,
    inverse_ref,
    q_ref,
    k_ref,
    p_ref,
    c_ref,
):
    slots, share, width = x1_ref.shape
    groups = share // GROUP
    rows = slots * GROUP
    times = times_ref[...].astype(f32)
    valid = jnp.where(times < info_ref[0:1, :slots], 1.0, 0.0)
    time = lax.broadcasted_iota(jnp.int32, (embed_ref.shape[0], slots), 0).astype(f32)
    lookup = jnp.where(time == times, 1.0, 0.0).astype(bf16)
    added = None
    for part in split_terms(embed_ref[...], 3):
        term = dot_tn(lookup, part)
        added = term if added is None else added + term
    valid_column = slot_columns(valid, rows)
    slot_index = lax.broadcasted_iota(jnp.int32, (slots, slots), 0)
    own_slot = slot_index == lax.broadcasted_iota(jnp.int32, (slots, slots), 1)
    valid_slots = jnp.sum(jnp.where(own_slot, valid, 0.0), axis=1, keepdims=True)
    chunk = 8
    all_rows = slots * share
    row_slot = lax.broadcasted_iota(jnp.int32, (slots, all_rows), 1) // share
    own_row = lax.broadcasted_iota(jnp.int32, (slots, all_rows), 0) == row_slot
    spread_rows = jnp.where(own_row, 1.0, 0.0).astype(bf16)
    valid_rows = jnp.broadcast_to(valid, (GROUP, slots)).astype(bf16)
    row_valid = dot_nn(valid_rows, spread_rows).astype(bf16)
    pooled = dot_nn(row_valid, x1_ref[...].reshape(all_rows, width))[:1]
    for slot in range(0, slots, GROUP):
        kept = valid_slots[slot : slot + GROUP] * added[slot : slot + GROUP]
        pooled = pooled + float(share) * jnp.sum(kept, axis=0, keepdims=True)
    for start in range(0, slots, chunk):
        y = x1_ref[start : start + chunk].astype(f32) + added[start : start + chunk][:, None, :]
        normed, inverse = normalize(y)
        for group in range(groups):
            own = slice(group * GROUP, (group + 1) * GROUP)
            at = pl.ds(group * rows + start * GROUP, chunk * GROUP)
            tn_ref[at, :] = normed[:, own, :].reshape(chunk * GROUP, width).astype(bf16)
            inverse_ref[at, :] = inverse[:, own, :].reshape(chunk * GROUP, 1)
    row_index = lax.broadcasted_iota(jnp.int32, (rows, rows), 0)
    column_index = lax.broadcasted_iota(jnp.int32, (rows, rows), 1)
    spread = jnp.where(
        lax.broadcasted_iota(jnp.int32, (slots, rows), 0)
        == lax.broadcasted_iota(jnp.int32, (slots, rows), 1) // GROUP,
        1.0,
        0.0,
    ).astype(bf16)
    key_valid = dot_nn(jnp.broadcast_to(valid, (GROUP, slots)).astype(bf16), spread)[:1]
    allowed = (row_index % GROUP == column_index % GROUP) & (key_valid > 0.5)
    for group in range(groups):
        at = pl.ds(group * rows, rows)
        packed = dot_nt(tn_ref[at, :], qkv_ref[: 2 * INNER, :])
        q_ref[at, :] = (packed[:, :INNER] * QUERY_SCALE).astype(bf16)
        k_ref[at, :] = packed[:, INNER:].astype(bf16)
        scores = []
        for head in range(HEADS):
            first, last, _ = window(head)
            query = keep_head(q_ref[at, first:last], head)
            scores.append(dot_nt(query, k_ref[at, first:last]))
        for head in range(HEADS):
            raised = jnp.where(allowed, jnp.exp2(scores[head]), 0.0)
            weights = raised * (valid_column / jnp.sum(raised, axis=-1, keepdims=True))
            p_ref[group, head] = weights.astype(bf16)
            c_ref[head : head + 1, at] = jnp.sum(weights, axis=0, keepdims=True)
    gathered = exact(dot_nn, c_ref[...], tn_ref[...])
    mixed_all = exact(dot_nt, gathered, qkv_ref[2 * INNER :, :])
    lane = lax.broadcasted_iota(jnp.int32, mixed_all.shape, 1)
    head_row = lax.broadcasted_iota(jnp.int32, mixed_all.shape, 0)
    own_lane = (lane >= head_row * HD) & (lane < head_row * HD + HD)
    mixed = jnp.sum(jnp.where(own_lane, mixed_all, 0.0), axis=0, keepdims=True)
    feature = pooled + exact(dot_nn, jnp.broadcast_to(mixed, (GROUP, INNER)), out_ref[...])[:1]
    z = exact(dot_nn, jnp.broadcast_to(feature, (GROUP, width)), proj_ref[...])[:1]
    z = z * info_ref[1:2, :1]
    embed_size = z.shape[1]
    send_ref[:, :, :embed_size] = jnp.broadcast_to(
        z[None], (send_ref.shape[0], 1, embed_size)
    )
    tiles = embed_size // LANES
    own_tile = lax.axis_index("frame") // (lax.axis_size("frame") // tiles)
    piece = jnp.zeros((1, LANES), f32)
    for tile in range(tiles):
        held = text_ref[:, tile * LANES : (tile + 1) * LANES]
        piece = jnp.where(own_tile == tile, held, piece)
    send_ref[:, :, embed_size:] = jnp.broadcast_to(piece[None], (send_ref.shape[0], 1, LANES))


def unit_rows(matrix):
    inverse = lax.rsqrt(jnp.sum(matrix * matrix, axis=-1, keepdims=True) + EPSILON)
    return matrix * inverse, inverse


def temporal_backward(
    batch,
    cotangent,
    info_ref,
    times_ref,
    parts_ref,
    tn_ref,
    inverse_ref,
    q_ref,
    k_ref,
    p_ref,
    c_ref,
    qkv_ref,
    out_ref,
    proj_ref,
    grad_ref,
    loss_ref,
    dtn_ref,
):
    slots, share, width = grad_ref.shape
    groups = share // GROUP
    rows = slots * GROUP
    clips = batch
    per_clip = parts_ref.shape[0] // clips
    embed_size = proj_ref.shape[1]
    parts = parts_ref[:, 0, :].reshape(per_clip, clips, parts_ref.shape[2])
    z = jnp.sum(parts[:, :, :embed_size], axis=0)
    tiles = embed_size // LANES
    text = jnp.concatenate(
        [parts[i * (per_clip // tiles), :, embed_size:] for i in range(tiles)], axis=1
    )
    e, inverse_z = unit_rows(z)
    u, _ = unit_rows(text)
    logits = (
        lax.dot_general(
            e,
            u,
            (((1,), (1,)), ((), ())),
            precision=lax.Precision.HIGHEST,
            preferred_element_type=f32,
        )
        * SHARPNESS
    )
    raised = jnp.exp(logits)
    row_total = jnp.sum(raised, axis=1, keepdims=True)
    column_total = jnp.sum(raised, axis=0, keepdims=True)
    diagonal = lax.broadcasted_iota(jnp.int32, logits.shape, 0) == lax.broadcasted_iota(
        jnp.int32, logits.shape, 1
    )
    loss = (
        0.5 * jnp.sum(jnp.log(row_total), axis=0, keepdims=True)
        + 0.5 * jnp.sum(jnp.log(column_total), axis=1, keepdims=True)
        - jnp.sum(jnp.sum(jnp.where(diagonal, logits, 0.0), axis=1, keepdims=True), axis=0, keepdims=True)
    )
    loss_ref[...] = jnp.broadcast_to(loss, loss_ref.shape)
    shares = 0.5 * (raised / row_total + raised / column_total) - jnp.where(diagonal, 1.0, 0.0)
    grad_e = (cotangent * SHARPNESS) * lax.dot_general(
        shares,
        u,
        (((1,), (0,)), ((), ())),
        precision=lax.Precision.HIGHEST,
        preferred_element_type=f32,
    )
    grad_z = inverse_z * (grad_e - e * jnp.sum(e * grad_e, axis=-1, keepdims=True))
    own = lax.broadcasted_iota(jnp.int32, grad_z.shape, 0) == lax.axis_index("batch")
    grad_own = jnp.sum(jnp.where(own, grad_z, 0.0), axis=0, keepdims=True)
    grad_own = grad_own * info_ref[1:2, :1]
    grad_feature = exact(dot_nt, jnp.broadcast_to(grad_own, grad_z.shape), proj_ref[...])
    grad_mixed = exact(dot_nt, grad_feature, out_ref[...])
    lane = lax.broadcasted_iota(jnp.int32, grad_mixed.shape, 1)
    head_row = lax.broadcasted_iota(jnp.int32, grad_mixed.shape, 0)
    own_lane = (lane >= head_row * HD) & (lane < head_row * HD + HD)
    value_grad = exact(dot_nn, jnp.where(own_lane, grad_mixed, 0.0), qkv_ref[2 * INNER :, :])
    high, low = split_terms(value_grad, 2)
    scores_grad = exact(dot_nt, value_grad, tn_ref[...])
    c_high, c_low = split_terms(c_ref[...], 2)
    times = times_ref[...].astype(f32)
    valid = jnp.where(times < info_ref[0:1, :slots], 1.0, 0.0)
    valid_column = slot_columns(valid, rows)
    for group in range(groups):
        at = pl.ds(group * rows, rows)
        grad_scores = []
        for head in range(HEADS):
            weights = p_ref[group, head].astype(f32)
            along = scores_grad[head : head + 1, group * rows : (group + 1) * rows]
            inner = jnp.sum(weights * along, axis=-1, keepdims=True)
            grad_scores.append((weights * (along - inner)).astype(bf16))
        dq, dk = [], []
        for head in range(HEADS):
            first, last, _ = window(head)
            dq.append(dot_nn(grad_scores[head], k_ref[at, first:last]))
        for head in range(HEADS):
            first, last, _ = window(head)
            dk.append(dot_tn(grad_scores[head], q_ref[at, first:last]))
        own = slice(group * rows, (group + 1) * rows)
        weights_c = jnp.concatenate([c_high[:, own], c_high[:, own], c_low[:, own]], axis=0)
        value_rows = jnp.concatenate([high, low, high], axis=0)
        grad_tn = dot_nn((merge_heads(dq) * SCALE).astype(bf16), qkv_ref[:INNER, :])
        grad_tn += dot_nn((merge_heads(dk) * KEY_BACK).astype(bf16), qkv_ref[INNER : 2 * INNER, :])
        dtn_ref[at, :] = grad_tn + dot_tn(weights_c, value_rows)
    chunk = 8
    for start in range(0, slots, chunk):
        pieces = []
        for group in range(groups):
            at = pl.ds(group * rows + start * GROUP, chunk * GROUP)
            back = normalize_back(dtn_ref[at, :], tn_ref[at, :].astype(f32), inverse_ref[at, :])
            back = (
                back
                + valid_column[start * GROUP : (start + chunk) * GROUP] * grad_feature[:1]
            )
            pieces.append(back.reshape(chunk, 1, GROUP, width))
        joined = jnp.concatenate(pieces, axis=1).reshape(chunk, share, width)
        grad_ref[start : start + chunk] = joined.astype(bf16)


def cost(microseconds):
    return pl.CostEstimate(flops=microseconds * 10**9, bytes_accessed=0, transcendentals=0)


def per_device(
    tokens,
    frame_time,
    valid_count,
    spatial_qkv,
    spatial_out,
    temporal_qkv,
    temporal_out,
    time_embed,
    video_proj,
    text_embed,
):
    frames_in = tokens[0]
    local_frames, patches, width = frames_in.shape
    owners = lax.axis_size("frame")
    clips = lax.axis_size("batch")
    devices = owners * clips
    share = patches // owners
    slots = owners * local_frames
    groups = share // GROUP
    rows = slots * share
    shape = jax.ShapeDtypeStruct
    traded = (owners, local_frames * share, width)
    params = pltpu.CompilerParams(vmem_limit_bytes=20 * MIB)
    spatial_qkv = spatial_qkv.T
    temporal_qkv = temporal_qkv.T
    xn, xn_inverse, info = pl.pallas_call(
        spatial_norm,
        out_shape=(
            shape(frames_in.shape, bf16),
            shape((local_frames, patches, 1), f32),
            shape((GROUP, LANES), f32),
        ),
        in_specs=[VMEM] * 2,
        out_specs=(VMEM,) * 3,
        compiler_params=params,
        cost_estimate=cost(30),
        name="spatial_norm",
    )(valid_count.reshape(1, 1), frames_in)
    part = shape((local_frames, patches, INNER), bf16)
    q, k, v, p, so = pl.pallas_call(
        spatial_attention,
        out_shape=(
            part,
            part,
            part,
            shape((local_frames, HEADS, patches, patches), bf16),
            part,
        ),
        in_specs=[VMEM] * 2,
        out_specs=(VMEM,) * 5,
        compiler_params=params,
        cost_estimate=cost(8),
        name="spatial_attention",
    )(xn, spatial_qkv)
    x1 = pl.pallas_call(
        spatial_output,
        out_shape=shape(traded, bf16),
        in_specs=[VMEM] * 3,
        out_specs=VMEM,
        compiler_params=params,
        cost_estimate=cost(2),
        name="spatial_output",
    )(frames_in, so, spatial_out)

    x1 = lax.all_to_all(x1, "frame", split_axis=0, concat_axis=0, tiled=True)
    x1 = x1.reshape(slots, share, width)
    embed_size = text_embed.shape[1]
    send, tn, inverse, tq, tk, tp, c = pl.pallas_call(
        temporal_forward,
        out_shape=(
            shape((devices, 1, embed_size + LANES), f32),
            shape((rows, width), bf16),
            shape((rows, 1), f32),
            shape((rows, INNER), bf16),
            shape((rows, INNER), bf16),
            shape((groups, HEADS, slots * GROUP, slots * GROUP), bf16),
            shape((HEADS, rows), f32),
        ),
        in_specs=[VMEM] * 8,
        out_specs=(VMEM,) * 7,
        compiler_params=params,
        cost_estimate=cost(7),
        name="temporal_forward",
    )(
        info,
        frame_time,
        x1,
        time_embed,
        temporal_qkv,
        temporal_out,
        video_proj,
        text_embed,
    )

    parts = lax.all_to_all(send, ("frame", "batch"), split_axis=0, concat_axis=0, tiled=True)
    grad_x1, loss = pl.pallas_call(
        functools.partial(temporal_backward, clips, float(slots * patches)),
        out_shape=(shape((slots, share, width), bf16), shape((GROUP, LANES), f32)),
        in_specs=[VMEM] * 12,
        out_specs=(VMEM,) * 2,
        scratch_shapes=[pltpu.VMEM((rows, width), f32)],
        compiler_params=params,
        cost_estimate=cost(8),
        name="temporal_backward",
    )(
        info,
        frame_time,
        parts,
        tn,
        inverse,
        tq,
        tk,
        tp,
        c,
        temporal_qkv,
        temporal_out,
        video_proj,
    )
    grad_x1 = lax.all_to_all(
        grad_x1.reshape(traded), "frame", split_axis=0, concat_axis=0, tiled=True
    )
    result, loss = pl.pallas_call(
        spatial_backward,
        out_shape=(shape(frames_in.shape, bf16), shape((1, 1), f32)),
        in_specs=[VMEM] * 11,
        out_specs=(HBM, HBM),
        scratch_shapes=[
            pltpu.VMEM(frames_in.shape, bf16),
            pltpu.VMEM((1, 1), f32),
            pltpu.SemaphoreType.DMA((local_frames, PIECES)),
            pltpu.SemaphoreType.DMA,
        ],
        compiler_params=params,
        cost_estimate=cost(12),
        name="spatial_backward",
    )(grad_x1, xn, xn_inverse, spatial_qkv, spatial_out, q, k, v, p, so, loss)
    return (result[None], loss[0, 0])


def solution(mesh):
    placed = (
        P("batch", "frame", None, None),
        P("batch", None),
        P("batch"),
        P(),
        P(),
        P(),
        P(),
        P(),
        P(),
        P("batch", None),
    )
    return jax.shard_map(
        per_device,
        mesh=mesh,
        in_specs=placed,
        out_specs=(P("batch", "frame", None, None), P()),
        check_vma=False,
    )
```

```python
import functools
import math

import jax
import jax.numpy as jnp
from jax import lax
from jax.experimental import pallas as pl
from jax.experimental.pallas import tpu as pltpu
from jax.sharding import PartitionSpec as P

HEADS = 8
HD = 88
INNER = HEADS * HD
LANES = 128
GROUP = 8
PIECES = 4
EPSILON = 1e-06
SHARPNESS = 1.0 / 0.07
SCALE = 1.0 / math.sqrt(HD)
QUERY_SCALE = SCALE / math.log(2.0)
KEY_BACK = math.log(2.0)
MIB = 1024 * 1024

bf16 = jnp.bfloat16
f32 = jnp.float32
VMEM = pl.BlockSpec(memory_space=pltpu.VMEM)
HBM = pl.BlockSpec(memory_space=pltpu.HBM)


def dot_nn(left, right):
    return lax.dot_general(left, right, (((1,), (0,)), ((), ())), preferred_element_type=f32)


def dot_nt(left, right):
    return lax.dot_general(left, right, (((1,), (1,)), ((), ())), preferred_element_type=f32)


def dot_tn(left, right):
    return lax.dot_general(left, right, (((0,), (0,)), ((), ())), preferred_element_type=f32)


def split_terms(values, terms):
    parts = []
    rest = values
    for _ in range(terms):
        part = rest.astype(bf16)
        parts.append(part)
        rest = rest - part.astype(f32)
    return parts


def exact(dot, values, matrix, terms=2):
    rows = values.shape[0]
    products = dot(jnp.concatenate(split_terms(values, terms), axis=0), matrix)
    total = products[:rows]
    for term in range(1, terms):
        total = total + products[term * rows : (term + 1) * rows]
    return total


def window(head):
    first = head * HD // LANES * LANES
    last = min(-(-(head + 1) * HD // LANES) * LANES, INNER)
    return first, last, head * HD - first


def head_lanes(rows, head):
    first, last, offset = window(head)
    lane = lax.broadcasted_iota(jnp.int32, (rows, last - first), 1)
    return (lane >= offset) & (lane < offset + HD)


def keep_head(values, head):
    return jnp.where(head_lanes(values.shape[0], head), values, jnp.zeros_like(values))


def merge_heads(products):
    tiles = []
    for start in range(0, INNER, LANES):
        width = min(LANES, INNER - start)
        tile = None
        for head in range(HEADS):
            first, last, offset = window(head)
            if first <= start < last:
                piece = products[head][:, start - first : start - first + width]
                if tile is None:
                    tile = piece
                else:
                    lane = lax.broadcasted_iota(jnp.int32, piece.shape, 1)
                    tile = jnp.where(lane >= head * HD - start, piece, tile)
        tiles.append(tile)
    return jnp.concatenate(tiles, axis=1)


def normalize(values):
    center = values - jnp.mean(values, axis=-1, keepdims=True)
    spread = jnp.mean(center * center, axis=-1, keepdims=True)
    inverse = lax.rsqrt(spread + EPSILON)
    return center * inverse, inverse


def normalize_back(grad, normed, inverse):
    return inverse * (
        grad
        - jnp.mean(grad, axis=-1, keepdims=True)
        - normed * jnp.mean(grad * normed, axis=-1, keepdims=True)
    )


def clip_info(patches, count_ref, info_ref):
    count = count_ref[...].astype(f32)
    info_ref[0:1, :] = jnp.broadcast_to(count, (1, info_ref.shape[1]))
    scale = 1.0 / (count * float(patches))
    info_ref[1:2, :] = jnp.broadcast_to(scale, (1, info_ref.shape[1]))


def spatial_norm(info_ref, tok_ref, xn_ref, inverse_ref):
    del info_ref
    for frame in range(tok_ref.shape[0]):
        normed, inverse = normalize(tok_ref[frame].astype(f32))
        xn_ref[frame] = normed.astype(bf16)
        inverse_ref[frame] = inverse


def spatial_attention(xn_ref, qkv_ref, q_ref, k_ref, v_ref, p_ref, so_ref):
    for frame in range(xn_ref.shape[0]):
        packed = dot_nt(xn_ref[frame], qkv_ref[...])
        q_ref[frame] = (packed[:, :INNER] * QUERY_SCALE).astype(bf16)
        k_ref[frame] = packed[:, INNER : 2 * INNER].astype(bf16)
        v_ref[frame] = packed[:, 2 * INNER :].astype(bf16)
        scores = []
        for head in range(HEADS):
            first, last, _ = window(head)
            query = keep_head(q_ref[frame, :, first:last], head)
            scores.append(dot_nt(query, k_ref[frame, :, first:last]))
        for head in range(HEADS):
            raised = jnp.exp2(scores[head])
            weights = raised * (1.0 / jnp.sum(raised, axis=-1, keepdims=True))
            p_ref[frame, head] = weights.astype(bf16)
        mixed = []
        for head in range(HEADS):
            first, last, _ = window(head)
            mixed.append(dot_nn(p_ref[frame, head], v_ref[frame, :, first:last]))
        so_ref[frame] = merge_heads(mixed).astype(bf16)


def spatial_output(tok_ref, so_ref, out_ref, x1_ref):
    frames, patches, width = tok_ref.shape
    owners = x1_ref.shape[0]
    share = patches // owners
    for frame in range(frames):
        update = dot_nn(so_ref[frame], out_ref[...])
        x1 = (tok_ref[frame].astype(f32) + update).astype(bf16)
        own = slice(frame * share, (frame + 1) * share)
        x1_ref[:, own, :] = x1.reshape(owners, share, width)


def spatial_backward(
    grad_ref,
    xn_ref,
    inverse_ref,
    qkv_ref,
    out_ref,
    q_ref,
    k_ref,
    v_ref,
    p_ref,
    so_ref,
    loss_ref,
    result_hbm,
    loss_hbm,
    result_ref,
    loss_held_ref,
    result_sem,
    loss_sem,
):
    loss_held_ref[...] = loss_ref[:1, :1]
    loss_copy = pltpu.make_async_copy(loss_held_ref, loss_hbm, loss_sem)
    loss_copy.start()
    frames, patches, width = xn_ref.shape
    owners = grad_ref.shape[0]
    share = patches // owners
    copies = []
    for frame in range(frames):
        own = slice(frame * share, (frame + 1) * share)
        grad_x1 = grad_ref[:, own, :].reshape(patches, width)
        grad_so = dot_nt(grad_x1, out_ref[...]).astype(bf16)
        dv = []
        for head in range(HEADS):
            first, last, _ = window(head)
            dv.append(dot_tn(p_ref[frame, head], grad_so[:, first:last]))
        dv = merge_heads(dv).astype(bf16)
        grad_weights, inner = [], []
        for head in range(HEADS):
            first, last, _ = window(head)
            grad_head = keep_head(grad_so[:, first:last], head)
            along = grad_head.astype(f32) * so_ref[frame, :, first:last].astype(f32)
            inner.append(jnp.sum(along, axis=-1, keepdims=True))
            grad_weights.append(dot_nt(grad_head, v_ref[frame, :, first:last]))
        dq, dk = [], []
        for head in range(HEADS):
            first, last, _ = window(head)
            weights = p_ref[frame, head].astype(f32)
            grad_scores = (weights * (grad_weights[head] - inner[head])).astype(bf16)
            dq.append(dot_nn(grad_scores, k_ref[frame, :, first:last]))
            dk.append(dot_tn(grad_scores, q_ref[frame, :, first:last]))
        grad_xn = dot_nn((merge_heads(dq) * SCALE).astype(bf16), qkv_ref[:INNER, :])
        grad_xn += dot_nn((merge_heads(dk) * KEY_BACK).astype(bf16), qkv_ref[INNER : 2 * INNER, :])
        grad_xn += dot_nn(dv, qkv_ref[2 * INNER :, :])
        for piece in range(PIECES):
            size = patches // PIECES
            at = slice(piece * size, (piece + 1) * size)
            back = normalize_back(
                grad_xn[at], xn_ref[frame, at].astype(f32), inverse_ref[frame, at]
            )
            held = slice(piece * owners // PIECES, (piece + 1) * owners // PIECES)
            grad_x1 = grad_ref[held, own, :].reshape(size, width)
            result_ref[frame, at] = (grad_x1.astype(f32) + back).astype(bf16)
            rows = pl.ds(piece * size, size)
            copy = pltpu.make_async_copy(
                result_ref.at[frame, rows],
                result_hbm.at[frame, rows],
                result_sem.at[frame, piece],
            )
            copy.start()
            copies.append(copy)
    for copy in copies + [loss_copy]:
        copy.wait()


def slot_columns(valid, rows):
    slots = valid.shape[1]
    row_slot = lax.broadcasted_iota(jnp.int32, (rows, slots), 0) // GROUP
    slot = lax.broadcasted_iota(jnp.int32, (rows, slots), 1)
    column = jnp.sum(jnp.where(row_slot == slot, valid, 0.0), axis=1, keepdims=True)
    return column


def temporal_forward(
    info_ref,
    times_ref,
    x1_ref,
    embed_ref,
    qkv_ref,
    out_ref,
    proj_ref,
    text_ref,
    send_ref,
    tn_ref,
    inverse_ref,
    q_ref,
    k_ref,
    p_ref,
    c_ref,
):
    slots, share, width = x1_ref.shape
    groups = share // GROUP
    rows = slots * GROUP
    times = times_ref[...].astype(f32)
    valid = jnp.where(times < info_ref[0:1, :slots], 1.0, 0.0)
    time = lax.broadcasted_iota(jnp.int32, (embed_ref.shape[0], slots), 0).astype(f32)
    lookup = jnp.where(time == times, 1.0, 0.0).astype(bf16)
    added = None
    for part in split_terms(embed_ref[...], 3):
        term = dot_tn(lookup, part)
        added = term if added is None else added + term
    valid_column = slot_columns(valid, rows)
    slot_index = lax.broadcasted_iota(jnp.int32, (slots, slots), 0)
    own_slot = slot_index == lax.broadcasted_iota(jnp.int32, (slots, slots), 1)
    valid_slots = jnp.sum(jnp.where(own_slot, valid, 0.0), axis=1, keepdims=True)
    chunk = 8
    all_rows = slots * share
    row_slot = lax.broadcasted_iota(jnp.int32, (slots, all_rows), 1) // share
    own_row = lax.broadcasted_iota(jnp.int32, (slots, all_rows), 0) == row_slot
    spread_rows = jnp.where(own_row, 1.0, 0.0).astype(bf16)
    valid_rows = jnp.broadcast_to(valid, (GROUP, slots)).astype(bf16)
    row_valid = dot_nn(valid_rows, spread_rows).astype(bf16)
    pooled = dot_nn(row_valid, x1_ref[...].reshape(all_rows, width))[:1]
    for slot in range(0, slots, GROUP):
        kept = valid_slots[slot : slot + GROUP] * added[slot : slot + GROUP]
        pooled = pooled + float(share) * jnp.sum(kept, axis=0, keepdims=True)
    for start in range(0, slots, chunk):
        y = x1_ref[start : start + chunk].astype(f32) + added[start : start + chunk][:, None, :]
        normed, inverse = normalize(y)
        for group in range(groups):
            own = slice(group * GROUP, (group + 1) * GROUP)
            at = pl.ds(group * rows + start * GROUP, chunk * GROUP)
            tn_ref[at, :] = normed[:, own, :].reshape(chunk * GROUP, width).astype(bf16)
            inverse_ref[at, :] = inverse[:, own, :].reshape(chunk * GROUP, 1)
    row_index = lax.broadcasted_iota(jnp.int32, (rows, rows), 0)
    column_index = lax.broadcasted_iota(jnp.int32, (rows, rows), 1)
    spread = jnp.where(
        lax.broadcasted_iota(jnp.int32, (slots, rows), 0)
        == lax.broadcasted_iota(jnp.int32, (slots, rows), 1) // GROUP,
        1.0,
        0.0,
    ).astype(bf16)
    key_valid = dot_nn(jnp.broadcast_to(valid, (GROUP, slots)).astype(bf16), spread)[:1]
    allowed = (row_index % GROUP == column_index % GROUP) & (key_valid > 0.5)
    for group in range(groups):
        at = pl.ds(group * rows, rows)
        packed = dot_nt(tn_ref[at, :], qkv_ref[: 2 * INNER, :])
        q_ref[at, :] = (packed[:, :INNER] * QUERY_SCALE).astype(bf16)
        k_ref[at, :] = packed[:, INNER:].astype(bf16)
        scores = []
        for head in range(HEADS):
            first, last, _ = window(head)
            query = keep_head(q_ref[at, first:last], head)
            scores.append(dot_nt(query, k_ref[at, first:last]))
        for head in range(HEADS):
            raised = jnp.where(allowed, jnp.exp2(scores[head]), 0.0)
            weights = raised * (valid_column / jnp.sum(raised, axis=-1, keepdims=True))
            p_ref[group, head] = weights.astype(bf16)
            c_ref[head : head + 1, at] = jnp.sum(weights, axis=0, keepdims=True)
    gathered = exact(dot_nn, c_ref[...], tn_ref[...])
    mixed_all = exact(dot_nt, gathered, qkv_ref[2 * INNER :, :])
    lane = lax.broadcasted_iota(jnp.int32, mixed_all.shape, 1)
    head_row = lax.broadcasted_iota(jnp.int32, mixed_all.shape, 0)
    own_lane = (lane >= head_row * HD) & (lane < head_row * HD + HD)
    mixed = jnp.sum(jnp.where(own_lane, mixed_all, 0.0), axis=0, keepdims=True)
    feature = pooled + exact(dot_nn, jnp.broadcast_to(mixed, (GROUP, INNER)), out_ref[...])[:1]
    z = exact(dot_nn, jnp.broadcast_to(feature, (GROUP, width)), proj_ref[...])[:1]
    z = z * info_ref[1:2, :1]
    embed_size = z.shape[1]
    send_ref[:, :, :embed_size] = jnp.broadcast_to(
        z[None], (send_ref.shape[0], 1, embed_size)
    )
    tiles = embed_size // LANES
    own_tile = lax.axis_index("frame") // (lax.axis_size("frame") // tiles)
    piece = jnp.zeros((1, LANES), f32)
    for tile in range(tiles):
        held = text_ref[:, tile * LANES : (tile + 1) * LANES]
        piece = jnp.where(own_tile == tile, held, piece)
    send_ref[:, :, embed_size:] = jnp.broadcast_to(piece[None], (send_ref.shape[0], 1, LANES))


def unit_rows(matrix):
    inverse = lax.rsqrt(jnp.sum(matrix * matrix, axis=-1, keepdims=True) + EPSILON)
    return matrix * inverse, inverse


def temporal_backward(
    batch,
    cotangent,
    info_ref,
    times_ref,
    parts_ref,
    tn_ref,
    inverse_ref,
    q_ref,
    k_ref,
    p_ref,
    c_ref,
    qkv_ref,
    out_ref,
    proj_ref,
    grad_ref,
    loss_ref,
    dtn_ref,
):
    slots, share, width = grad_ref.shape
    groups = share // GROUP
    rows = slots * GROUP
    clips = batch
    per_clip = parts_ref.shape[0] // clips
    embed_size = proj_ref.shape[1]
    parts = parts_ref[:, 0, :].reshape(per_clip, clips, parts_ref.shape[2])
    z = jnp.sum(parts[:, :, :embed_size], axis=0)
    tiles = embed_size // LANES
    text = jnp.concatenate(
        [parts[i * (per_clip // tiles), :, embed_size:] for i in range(tiles)], axis=1
    )
    e, inverse_z = unit_rows(z)
    u, _ = unit_rows(text)
    logits = (
        lax.dot_general(
            e,
            u,
            (((1,), (1,)), ((), ())),
            precision=lax.Precision.HIGHEST,
            preferred_element_type=f32,
        )
        * SHARPNESS
    )
    raised = jnp.exp(logits)
    row_total = jnp.sum(raised, axis=1, keepdims=True)
    column_total = jnp.sum(raised, axis=0, keepdims=True)
    diagonal = lax.broadcasted_iota(jnp.int32, logits.shape, 0) == lax.broadcasted_iota(
        jnp.int32, logits.shape, 1
    )
    loss = (
        0.5 * jnp.sum(jnp.log(row_total), axis=0, keepdims=True)
        + 0.5 * jnp.sum(jnp.log(column_total), axis=1, keepdims=True)
        - jnp.sum(jnp.sum(jnp.where(diagonal, logits, 0.0), axis=1, keepdims=True), axis=0, keepdims=True)
    )
    loss_ref[...] = jnp.broadcast_to(loss, loss_ref.shape)
    shares = 0.5 * (raised / row_total + raised / column_total) - jnp.where(diagonal, 1.0, 0.0)
    grad_e = (cotangent * SHARPNESS) * lax.dot_general(
        shares,
        u,
        (((1,), (0,)), ((), ())),
        precision=lax.Precision.HIGHEST,
        preferred_element_type=f32,
    )
    grad_z = inverse_z * (grad_e - e * jnp.sum(e * grad_e, axis=-1, keepdims=True))
    own = lax.broadcasted_iota(jnp.int32, grad_z.shape, 0) == lax.axis_index("batch")
    grad_own = jnp.sum(jnp.where(own, grad_z, 0.0), axis=0, keepdims=True)
    grad_own = grad_own * info_ref[1:2, :1]
    grad_feature = exact(dot_nt, jnp.broadcast_to(grad_own, grad_z.shape), proj_ref[...])
    grad_mixed = exact(dot_nt, grad_feature, out_ref[...])
    lane = lax.broadcasted_iota(jnp.int32, grad_mixed.shape, 1)
    head_row = lax.broadcasted_iota(jnp.int32, grad_mixed.shape, 0)
    own_lane = (lane >= head_row * HD) & (lane < head_row * HD + HD)
    value_grad = exact(dot_nn, jnp.where(own_lane, grad_mixed, 0.0), qkv_ref[2 * INNER :, :])
    high, low = split_terms(value_grad, 2)
    scores_grad = exact(dot_nt, value_grad, tn_ref[...])
    c_high, c_low = split_terms(c_ref[...], 2)
    times = times_ref[...].astype(f32)
    valid = jnp.where(times < info_ref[0:1, :slots], 1.0, 0.0)
    valid_column = slot_columns(valid, rows)
    for group in range(groups):
        at = pl.ds(group * rows, rows)
        grad_scores = []
        for head in range(HEADS):
            weights = p_ref[group, head].astype(f32)
            along = scores_grad[head : head + 1, group * rows : (group + 1) * rows]
            inner = jnp.sum(weights * along, axis=-1, keepdims=True)
            grad_scores.append((weights * (along - inner)).astype(bf16))
        dq, dk = [], []
        for head in range(HEADS):
            first, last, _ = window(head)
            dq.append(dot_nn(grad_scores[head], k_ref[at, first:last]))
        for head in range(HEADS):
            first, last, _ = window(head)
            dk.append(dot_tn(grad_scores[head], q_ref[at, first:last]))
        own = slice(group * rows, (group + 1) * rows)
        weights_c = jnp.concatenate([c_high[:, own], c_high[:, own], c_low[:, own]], axis=0)
        value_rows = jnp.concatenate([high, low, high], axis=0)
        grad_tn = dot_nn((merge_heads(dq) * SCALE).astype(bf16), qkv_ref[:INNER, :])
        grad_tn += dot_nn((merge_heads(dk) * KEY_BACK).astype(bf16), qkv_ref[INNER : 2 * INNER, :])
        dtn_ref[at, :] = grad_tn + dot_tn(weights_c, value_rows)
    chunk = 8
    for start in range(0, slots, chunk):
        pieces = []
        for group in range(groups):
            at = pl.ds(group * rows + start * GROUP, chunk * GROUP)
            back = normalize_back(dtn_ref[at, :], tn_ref[at, :].astype(f32), inverse_ref[at, :])
            back = (
                back
                + valid_column[start * GROUP : (start + chunk) * GROUP] * grad_feature[:1]
            )
            pieces.append(back.reshape(chunk, 1, GROUP, width))
        joined = jnp.concatenate(pieces, axis=1).reshape(chunk, share, width)
        grad_ref[start : start + chunk] = joined.astype(bf16)


def cost(microseconds):
    return pl.CostEstimate(flops=microseconds * 10**9, bytes_accessed=0, transcendentals=0)


def per_device(
    tokens,
    frame_time,
    valid_count,
    spatial_qkv,
    spatial_out,
    temporal_qkv,
    temporal_out,
    time_embed,
    video_proj,
    text_embed,
):
    frames_in = tokens[0]
    local_frames, patches, width = frames_in.shape
    owners = lax.axis_size("frame")
    clips = lax.axis_size("batch")
    devices = owners * clips
    share = patches // owners
    slots = owners * local_frames
    groups = share // GROUP
    rows = slots * share
    shape = jax.ShapeDtypeStruct
    traded = (owners, local_frames * share, width)
    params = pltpu.CompilerParams(vmem_limit_bytes=20 * MIB)
    spatial_qkv = spatial_qkv.T
    temporal_qkv = temporal_qkv.T
    info = pl.pallas_call(
        functools.partial(clip_info, patches),
        out_shape=shape((GROUP, LANES), f32),
        in_specs=[VMEM],
        out_specs=VMEM,
        compiler_params=params,
        cost_estimate=cost(30),
        name="clip_info",
    )(valid_count.reshape(1, 1))
    xn, xn_inverse = pl.pallas_call(
        spatial_norm,
        out_shape=(
            shape(frames_in.shape, bf16),
            shape((local_frames, patches, 1), f32),
        ),
        in_specs=[VMEM] * 2,
        out_specs=(VMEM,) * 2,
        compiler_params=params,
        cost_estimate=cost(2),
        name="spatial_norm",
    )(info, frames_in)
    part = shape((local_frames, patches, INNER), bf16)
    q, k, v, p, so = pl.pallas_call(
        spatial_attention,
        out_shape=(
            part,
            part,
            part,
            shape((local_frames, HEADS, patches, patches), bf16),
            part,
        ),
        in_specs=[VMEM] * 2,
        out_specs=(VMEM,) * 5,
        compiler_params=params,
        cost_estimate=cost(30),
        name="spatial_attention",
    )(xn, spatial_qkv)
    x1 = pl.pallas_call(
        spatial_output,
        out_shape=shape(traded, bf16),
        in_specs=[VMEM] * 3,
        out_specs=VMEM,
        compiler_params=params,
        cost_estimate=cost(2),
        name="spatial_output",
    )(frames_in, so, spatial_out)

    x1 = lax.all_to_all(x1, "frame", split_axis=0, concat_axis=0, tiled=True)
    x1 = x1.reshape(slots, share, width)
    embed_size = text_embed.shape[1]
    send, tn, inverse, tq, tk, tp, c = pl.pallas_call(
        temporal_forward,
        out_shape=(
            shape((devices, 1, embed_size + LANES), f32),
            shape((rows, width), bf16),
            shape((rows, 1), f32),
            shape((rows, INNER), bf16),
            shape((rows, INNER), bf16),
            shape((groups, HEADS, slots * GROUP, slots * GROUP), bf16),
            shape((HEADS, rows), f32),
        ),
        in_specs=[VMEM] * 8,
        out_specs=(VMEM,) * 7,
        compiler_params=params,
        cost_estimate=cost(7),
        name="temporal_forward",
    )(
        info,
        frame_time,
        x1,
        time_embed,
        temporal_qkv,
        temporal_out,
        video_proj,
        text_embed,
    )

    parts = lax.all_to_all(send, ("frame", "batch"), split_axis=0, concat_axis=0, tiled=True)
    grad_x1, loss = pl.pallas_call(
        functools.partial(temporal_backward, clips, float(slots * patches)),
        out_shape=(shape((slots, share, width), bf16), shape((GROUP, LANES), f32)),
        in_specs=[VMEM] * 12,
        out_specs=(VMEM,) * 2,
        scratch_shapes=[pltpu.VMEM((rows, width), f32)],
        compiler_params=params,
        cost_estimate=cost(8),
        name="temporal_backward",
    )(
        info,
        frame_time,
        parts,
        tn,
        inverse,
        tq,
        tk,
        tp,
        c,
        temporal_qkv,
        temporal_out,
        video_proj,
    )
    grad_x1 = lax.all_to_all(
        grad_x1.reshape(traded), "frame", split_axis=0, concat_axis=0, tiled=True
    )
    result, loss = pl.pallas_call(
        spatial_backward,
        out_shape=(shape(frames_in.shape, bf16), shape((1, 1), f32)),
        in_specs=[VMEM] * 11,
        out_specs=(HBM, HBM),
        scratch_shapes=[
            pltpu.VMEM(frames_in.shape, bf16),
            pltpu.VMEM((1, 1), f32),
            pltpu.SemaphoreType.DMA((local_frames, PIECES)),
            pltpu.SemaphoreType.DMA,
        ],
        compiler_params=params,
        cost_estimate=cost(12),
        name="spatial_backward",
    )(grad_x1, xn, xn_inverse, spatial_qkv, spatial_out, q, k, v, p, so, loss)
    return (result[None], loss[0, 0])


def solution(mesh):
    placed = (
        P("batch", "frame", None, None),
        P("batch", None),
        P("batch"),
        P(),
        P(),
        P(),
        P(),
        P(),
        P(),
        P("batch", None),
    )
    return jax.shard_map(
        per_device,
        mesh=mesh,
        in_specs=placed,
        out_specs=(P("batch", "frame", None, None), P()),
        check_vma=False,
    )
```

```python
import functools
import math

import jax
import jax.numpy as jnp
from jax import lax
from jax.experimental import pallas as pl
from jax.experimental.pallas import tpu as pltpu
from jax.sharding import PartitionSpec as P

HEADS = 8
HD = 88
INNER = HEADS * HD
LANES = 128
GROUP = 8
SPLIT = 512
PIECES = 4
EPSILON = 1e-06
SHARPNESS = 1.0 / 0.07
SCALE = 1.0 / math.sqrt(HD)
QUERY_SCALE = SCALE / math.log(2.0)
KEY_BACK = math.log(2.0)
MIB = 1024 * 1024

bf16 = jnp.bfloat16
f32 = jnp.float32
VMEM = pl.BlockSpec(memory_space=pltpu.VMEM)
HBM = pl.BlockSpec(memory_space=pltpu.HBM)


def dot_nn(left, right):
    return lax.dot_general(left, right, (((1,), (0,)), ((), ())), preferred_element_type=f32)


def dot_nt(left, right):
    return lax.dot_general(left, right, (((1,), (1,)), ((), ())), preferred_element_type=f32)


def dot_tn(left, right):
    return lax.dot_general(left, right, (((0,), (0,)), ((), ())), preferred_element_type=f32)


def split_terms(values, terms):
    parts = []
    rest = values
    for _ in range(terms):
        part = rest.astype(bf16)
        parts.append(part)
        rest = rest - part.astype(f32)
    return parts


def exact(dot, values, matrix, terms=2):
    rows = values.shape[0]
    products = dot(jnp.concatenate(split_terms(values, terms), axis=0), matrix)
    total = products[:rows]
    for term in range(1, terms):
        total = total + products[term * rows : (term + 1) * rows]
    return total


def window(head):
    first = head * HD // LANES * LANES
    last = min(-(-(head + 1) * HD // LANES) * LANES, INNER)
    return first, last, head * HD - first


def head_lanes(rows, head):
    first, last, offset = window(head)
    lane = lax.broadcasted_iota(jnp.int32, (rows, last - first), 1)
    return (lane >= offset) & (lane < offset + HD)


def keep_head(values, head):
    return jnp.where(head_lanes(values.shape[0], head), values, jnp.zeros_like(values))


def merge_heads(products):
    tiles = []
    for start in range(0, INNER, LANES):
        width = min(LANES, INNER - start)
        tile = None
        for head in range(HEADS):
            first, last, offset = window(head)
            if first <= start < last:
                piece = products[head][:, start - first : start - first + width]
                if tile is None:
                    tile = piece
                else:
                    lane = lax.broadcasted_iota(jnp.int32, piece.shape, 1)
                    tile = jnp.where(lane >= head * HD - start, piece, tile)
        tiles.append(tile)
    return jnp.concatenate(tiles, axis=1)


def normalize(values):
    center = values - jnp.mean(values, axis=-1, keepdims=True)
    spread = jnp.mean(center * center, axis=-1, keepdims=True)
    inverse = lax.rsqrt(spread + EPSILON)
    return center * inverse, inverse


def normalize_back(grad, normed, inverse):
    return inverse * (
        grad
        - jnp.mean(grad, axis=-1, keepdims=True)
        - normed * jnp.mean(grad * normed, axis=-1, keepdims=True)
    )


def clip_info(patches, count_ref, info_ref):
    count = count_ref[...].astype(f32)
    info_ref[0:1, :] = jnp.broadcast_to(count, (1, info_ref.shape[1]))
    scale = 1.0 / (count * float(patches))
    info_ref[1:2, :] = jnp.broadcast_to(scale, (1, info_ref.shape[1]))


def spatial_norm(info_ref, tok_ref, xn_ref, inverse_ref):
    del info_ref
    for frame in range(tok_ref.shape[0]):
        normed, inverse = normalize(tok_ref[frame].astype(f32))
        xn_ref[frame] = normed.astype(bf16)
        inverse_ref[frame] = inverse


def spatial_attention(xn_ref, qkv_ref, q_ref, k_ref, v_ref, p_ref, so_ref):
    for frame in range(xn_ref.shape[0]):
        packed = dot_nt(xn_ref[frame], qkv_ref[...])
        q_ref[frame] = (packed[:, :INNER] * QUERY_SCALE).astype(bf16)
        k_ref[frame] = packed[:, INNER : 2 * INNER].astype(bf16)
        v_ref[frame] = packed[:, 2 * INNER :].astype(bf16)
        scores = []
        for head in range(HEADS):
            first, last, _ = window(head)
            query = keep_head(q_ref[frame, :, first:last], head)
            scores.append(dot_nt(query, k_ref[frame, :, first:last]))
        for head in range(HEADS):
            raised = jnp.exp2(scores[head])
            weights = raised * (1.0 / jnp.sum(raised, axis=-1, keepdims=True))
            p_ref[frame, head] = weights.astype(bf16)
        mixed = []
        for head in range(HEADS):
            first, last, _ = window(head)
            mixed.append(dot_nn(p_ref[frame, head], v_ref[frame, :, first:last]))
        so_ref[frame] = merge_heads(mixed).astype(bf16)


def spatial_output(tok_ref, so_ref, out_ref, x1_ref):
    frames, patches, width = tok_ref.shape
    owners = x1_ref.shape[0]
    share = patches // owners
    for frame in range(frames):
        update = dot_nn(so_ref[frame], out_ref[...])
        x1 = (tok_ref[frame].astype(f32) + update).astype(bf16)
        own = slice(frame * share, (frame + 1) * share)
        x1_ref[:, own, :] = x1.reshape(owners, share, width)


def spatial_backward(
    grad_ref,
    xn_ref,
    inverse_ref,
    qkv_ref,
    out_ref,
    q_ref,
    k_ref,
    v_ref,
    p_ref,
    so_ref,
    loss_ref,
    result_hbm,
    loss_hbm,
    result_ref,
    loss_held_ref,
    result_sem,
    loss_sem,
):
    loss_held_ref[...] = loss_ref[:1, :1]
    loss_copy = pltpu.make_async_copy(loss_held_ref, loss_hbm, loss_sem)
    loss_copy.start()
    frames, patches, width = xn_ref.shape
    owners = grad_ref.shape[0]
    share = patches // owners
    copies = []
    for frame in range(frames):
        own = slice(frame * share, (frame + 1) * share)
        grad_x1 = grad_ref[:, own, :].reshape(patches, width)
        grad_so = dot_nt(grad_x1, out_ref[...]).astype(bf16)
        dv = []
        for head in range(HEADS):
            first, last, _ = window(head)
            dv.append(dot_tn(p_ref[frame, head], grad_so[:, first:last]))
        dv = merge_heads(dv).astype(bf16)
        grad_weights, inner = [], []
        for head in range(HEADS):
            first, last, _ = window(head)
            grad_head = keep_head(grad_so[:, first:last], head)
            along = grad_head.astype(f32) * so_ref[frame, :, first:last].astype(f32)
            inner.append(jnp.sum(along, axis=-1, keepdims=True))
            grad_weights.append(dot_nt(grad_head, v_ref[frame, :, first:last]))
        dq, dk = [], []
        for head in range(HEADS):
            first, last, _ = window(head)
            weights = p_ref[frame, head].astype(f32)
            grad_scores = (weights * (grad_weights[head] - inner[head])).astype(bf16)
            dq.append(dot_nn(grad_scores, k_ref[frame, :, first:last]))
            dk.append(dot_tn(grad_scores, q_ref[frame, :, first:last]))
        grad_xn = dot_nn((merge_heads(dq) * SCALE).astype(bf16), qkv_ref[:INNER, :])
        grad_xn += dot_nn((merge_heads(dk) * KEY_BACK).astype(bf16), qkv_ref[INNER : 2 * INNER, :])
        grad_xn += dot_nn(dv, qkv_ref[2 * INNER :, :])
        for piece in range(PIECES):
            size = patches // PIECES
            at = slice(piece * size, (piece + 1) * size)
            back = normalize_back(
                grad_xn[at], xn_ref[frame, at].astype(f32), inverse_ref[frame, at]
            )
            held = slice(piece * owners // PIECES, (piece + 1) * owners // PIECES)
            grad_x1 = grad_ref[held, own, :].reshape(size, width)
            result_ref[frame, at] = (grad_x1.astype(f32) + back).astype(bf16)
            rows = pl.ds(piece * size, size)
            copy = pltpu.make_async_copy(
                result_ref.at[frame, rows],
                result_hbm.at[frame, rows],
                result_sem.at[frame, piece],
            )
            copy.start()
            copies.append(copy)
    for copy in copies + [loss_copy]:
        copy.wait()


def slot_columns(valid, rows):
    slots = valid.shape[1]
    row_slot = lax.broadcasted_iota(jnp.int32, (rows, slots), 0) // GROUP
    slot = lax.broadcasted_iota(jnp.int32, (rows, slots), 1)
    column = jnp.sum(jnp.where(row_slot == slot, valid, 0.0), axis=1, keepdims=True)
    return column


def temporal_forward(
    info_ref,
    times_ref,
    x1_ref,
    embed_ref,
    qkv_ref,
    out_ref,
    proj_ref,
    text_ref,
    send_ref,
    tn_ref,
    inverse_ref,
    q_ref,
    k_ref,
    p_ref,
    c_ref,
):
    slots, share, width = x1_ref.shape
    groups = share // GROUP
    rows = slots * GROUP
    times = times_ref[...].astype(f32)
    valid = jnp.where(times < info_ref[0:1, :slots], 1.0, 0.0)
    time = lax.broadcasted_iota(jnp.int32, (embed_ref.shape[0], slots), 0).astype(f32)
    lookup = jnp.where(time == times, 1.0, 0.0).astype(bf16)
    added = None
    for part in split_terms(embed_ref[...], 3):
        term = dot_tn(lookup, part)
        added = term if added is None else added + term
    valid_column = slot_columns(valid, rows)
    slot_index = lax.broadcasted_iota(jnp.int32, (slots, slots), 0)
    own_slot = slot_index == lax.broadcasted_iota(jnp.int32, (slots, slots), 1)
    valid_slots = jnp.sum(jnp.where(own_slot, valid, 0.0), axis=1, keepdims=True)
    chunk = 8
    all_rows = slots * share
    row_slot = lax.broadcasted_iota(jnp.int32, (slots, all_rows), 1) // share
    own_row = lax.broadcasted_iota(jnp.int32, (slots, all_rows), 0) == row_slot
    spread_rows = jnp.where(own_row, 1.0, 0.0).astype(bf16)
    valid_rows = jnp.broadcast_to(valid, (GROUP, slots)).astype(bf16)
    row_valid = dot_nn(valid_rows, spread_rows).astype(bf16)
    pooled = dot_nn(row_valid, x1_ref[...].reshape(all_rows, width))[:1]
    for slot in range(0, slots, GROUP):
        kept = valid_slots[slot : slot + GROUP] * added[slot : slot + GROUP]
        pooled = pooled + float(share) * jnp.sum(kept, axis=0, keepdims=True)
    for start in range(0, slots, chunk):
        y = x1_ref[start : start + chunk].astype(f32) + added[start : start + chunk][:, None, :]
        normed, inverse = normalize(y)
        for group in range(groups):
            own = slice(group * GROUP, (group + 1) * GROUP)
            at = pl.ds(group * rows + start * GROUP, chunk * GROUP)
            tn_ref[at, :] = normed[:, own, :].reshape(chunk * GROUP, width).astype(bf16)
            inverse_ref[at, :] = inverse[:, own, :].reshape(chunk * GROUP, 1)
    row_index = lax.broadcasted_iota(jnp.int32, (rows, rows), 0)
    column_index = lax.broadcasted_iota(jnp.int32, (rows, rows), 1)
    spread = jnp.where(
        lax.broadcasted_iota(jnp.int32, (slots, rows), 0)
        == lax.broadcasted_iota(jnp.int32, (slots, rows), 1) // GROUP,
        1.0,
        0.0,
    ).astype(bf16)
    key_valid = dot_nn(jnp.broadcast_to(valid, (GROUP, slots)).astype(bf16), spread)[:1]
    allowed = (row_index % GROUP == column_index % GROUP) & (key_valid > 0.5)
    for group in range(groups):
        at = pl.ds(group * rows, rows)
        packed = dot_nt(tn_ref[at, :], qkv_ref[: 2 * INNER, :])
        q_ref[at, :] = (packed[:, :INNER] * QUERY_SCALE).astype(bf16)
        k_ref[at, :] = packed[:, INNER:].astype(bf16)
        scores = []
        for head in range(HEADS):
            first, last, _ = window(head)
            query = keep_head(q_ref[at, first:last], head)
            scores.append(dot_nt(query, k_ref[at, first:last]))
        for head in range(HEADS):
            raised = jnp.where(allowed, jnp.exp2(scores[head]), 0.0)
            weights = raised * (valid_column / jnp.sum(raised, axis=-1, keepdims=True))
            p_ref[group, head] = weights.astype(bf16)
            c_ref[head : head + 1, at] = jnp.sum(weights, axis=0, keepdims=True)
    gathered = exact(dot_nn, c_ref[...], tn_ref[...])
    mixed_all = exact(dot_nt, gathered, qkv_ref[2 * INNER :, :])
    lane = lax.broadcasted_iota(jnp.int32, mixed_all.shape, 1)
    head_row = lax.broadcasted_iota(jnp.int32, mixed_all.shape, 0)
    own_lane = (lane >= head_row * HD) & (lane < head_row * HD + HD)
    mixed = jnp.sum(jnp.where(own_lane, mixed_all, 0.0), axis=0, keepdims=True)
    feature = pooled + exact(dot_nn, jnp.broadcast_to(mixed, (GROUP, INNER)), out_ref[...])[:1]
    z = exact(dot_nn, jnp.broadcast_to(feature, (GROUP, width)), proj_ref[...])[:1]
    z = z * info_ref[1:2, :1]
    embed_size = z.shape[1]
    send_ref[:, :, :embed_size] = jnp.broadcast_to(
        z[None], (send_ref.shape[0], 1, embed_size)
    )
    tiles = embed_size // LANES
    own_tile = lax.axis_index("frame") // (lax.axis_size("frame") // tiles)
    piece = jnp.zeros((1, LANES), f32)
    for tile in range(tiles):
        held = text_ref[:, tile * LANES : (tile + 1) * LANES]
        piece = jnp.where(own_tile == tile, held, piece)
    send_ref[:, :, embed_size:] = jnp.broadcast_to(piece[None], (send_ref.shape[0], 1, LANES))


def unit_rows(matrix):
    inverse = lax.rsqrt(jnp.sum(matrix * matrix, axis=-1, keepdims=True) + EPSILON)
    return matrix * inverse, inverse


def temporal_backward(
    batch,
    cotangent,
    info_ref,
    times_ref,
    parts_ref,
    tn_ref,
    inverse_ref,
    q_ref,
    k_ref,
    p_ref,
    c_ref,
    qkv_ref,
    out_ref,
    proj_ref,
    grad_ref,
    loss_ref,
    dtn_ref,
):
    slots, share, width = grad_ref.shape
    groups = share // GROUP
    rows = slots * GROUP
    clips = batch
    per_clip = parts_ref.shape[0] // clips
    embed_size = proj_ref.shape[1]
    parts = parts_ref[:, 0, :].reshape(per_clip, clips, parts_ref.shape[2])
    z = jnp.sum(parts[:, :, :embed_size], axis=0)
    tiles = embed_size // LANES
    text = jnp.concatenate(
        [parts[i * (per_clip // tiles), :, embed_size:] for i in range(tiles)], axis=1
    )
    e, inverse_z = unit_rows(z)
    u, _ = unit_rows(text)
    column = lax.broadcasted_iota(jnp.int32, (clips, clips), 1)
    logits = jnp.zeros((clips, clips), f32)
    for j in range(clips):
        product = jnp.sum(e * u[j : j + 1], axis=1, keepdims=True) * SHARPNESS
        logits = jnp.where(column == j, product, logits)
    raised = jnp.exp(logits)
    row_total = jnp.sum(raised, axis=1, keepdims=True)
    column_total = jnp.sum(raised, axis=0, keepdims=True)
    diagonal = lax.broadcasted_iota(jnp.int32, logits.shape, 0) == lax.broadcasted_iota(
        jnp.int32, logits.shape, 1
    )
    loss = (
        0.5 * jnp.sum(jnp.log(row_total), axis=0, keepdims=True)
        + 0.5 * jnp.sum(jnp.log(column_total), axis=1, keepdims=True)
        - jnp.sum(jnp.sum(jnp.where(diagonal, logits, 0.0), axis=1, keepdims=True), axis=0, keepdims=True)
    )
    loss_ref[...] = jnp.broadcast_to(loss, loss_ref.shape)
    shares = 0.5 * (raised / row_total + raised / column_total) - jnp.where(diagonal, 1.0, 0.0)
    shares = shares * (cotangent * SHARPNESS)
    grad_e = shares[:, 0:1] * u[0:1]
    for j in range(1, clips):
        grad_e = grad_e + shares[:, j : j + 1] * u[j : j + 1]
    grad_z = inverse_z * (grad_e - e * jnp.sum(e * grad_e, axis=-1, keepdims=True))
    own = lax.broadcasted_iota(jnp.int32, grad_z.shape, 0) == lax.axis_index("batch")
    grad_own = jnp.sum(jnp.where(own, grad_z, 0.0), axis=0, keepdims=True)
    grad_own = grad_own * info_ref[1:2, :1]
    grad_feature = exact(dot_nt, jnp.broadcast_to(grad_own, grad_z.shape), proj_ref[...])
    grad_mixed = exact(dot_nt, grad_feature, out_ref[...])
    lane = lax.broadcasted_iota(jnp.int32, grad_mixed.shape, 1)
    head_row = lax.broadcasted_iota(jnp.int32, grad_mixed.shape, 0)
    own_lane = (lane >= head_row * HD) & (lane < head_row * HD + HD)
    value_grad = exact(dot_nn, jnp.where(own_lane, grad_mixed, 0.0), qkv_ref[2 * INNER :, :])
    high, low = split_terms(value_grad, 2)
    scores_grad = exact(dot_nt, value_grad, tn_ref[...])
    c_high, c_low = split_terms(c_ref[...], 2)
    times = times_ref[...].astype(f32)
    valid = jnp.where(times < info_ref[0:1, :slots], 1.0, 0.0)
    valid_column = slot_columns(valid, rows)
    for group in range(groups):
        at = pl.ds(group * rows, rows)
        grad_scores = []
        for head in range(HEADS):
            weights = p_ref[group, head].astype(f32)
            along = scores_grad[head : head + 1, group * rows : (group + 1) * rows]
            inner = jnp.sum(weights * along, axis=-1, keepdims=True)
            grad_scores.append((weights * (along - inner)).astype(bf16))
        dq, dk = [], []
        for head in range(HEADS):
            first, last, _ = window(head)
            dq.append(dot_nn(grad_scores[head], k_ref[at, first:last]))
        for head in range(HEADS):
            first, last, _ = window(head)
            dk.append(dot_tn(grad_scores[head], q_ref[at, first:last]))
        own = slice(group * rows, (group + 1) * rows)
        weights_c = jnp.concatenate([c_high[:, own], c_high[:, own], c_low[:, own]], axis=0)
        value_rows = jnp.concatenate([high, low, high], axis=0)
        grad_tn = dot_nn((merge_heads(dq) * SCALE).astype(bf16), qkv_ref[:INNER, :])
        dk = (merge_heads(dk) * KEY_BACK).astype(bf16)
        grad_tn += dot_nn(dk[:, :SPLIT], qkv_ref[INNER : INNER + SPLIT, :])
        last = jnp.concatenate([dk[:, SPLIT:], weights_c.astype(f32).T.astype(bf16)], axis=1)
        rest_rows = jnp.concatenate([qkv_ref[INNER + SPLIT : 2 * INNER, :], value_rows], axis=0)
        dtn_ref[at, :] = grad_tn + dot_nn(last, rest_rows)
    chunk = 8
    for start in range(0, slots, chunk):
        pieces = []
        for group in range(groups):
            at = pl.ds(group * rows + start * GROUP, chunk * GROUP)
            back = normalize_back(dtn_ref[at, :], tn_ref[at, :].astype(f32), inverse_ref[at, :])
            back = (
                back
                + valid_column[start * GROUP : (start + chunk) * GROUP] * grad_feature[:1]
            )
            pieces.append(back.reshape(chunk, 1, GROUP, width))
        joined = jnp.concatenate(pieces, axis=1).reshape(chunk, share, width)
        grad_ref[start : start + chunk] = joined.astype(bf16)


def cost(microseconds):
    return pl.CostEstimate(flops=microseconds * 10**9, bytes_accessed=0, transcendentals=0)


def per_device(
    tokens,
    frame_time,
    valid_count,
    spatial_qkv,
    spatial_out,
    temporal_qkv,
    temporal_out,
    time_embed,
    video_proj,
    text_embed,
):
    frames_in = tokens[0]
    local_frames, patches, width = frames_in.shape
    owners = lax.axis_size("frame")
    clips = lax.axis_size("batch")
    devices = owners * clips
    share = patches // owners
    slots = owners * local_frames
    groups = share // GROUP
    rows = slots * share
    shape = jax.ShapeDtypeStruct
    traded = (owners, local_frames * share, width)
    params = pltpu.CompilerParams(vmem_limit_bytes=20 * MIB)
    spatial_qkv = spatial_qkv.T
    temporal_qkv = temporal_qkv.T
    info = pl.pallas_call(
        functools.partial(clip_info, patches),
        out_shape=shape((GROUP, LANES), f32),
        in_specs=[VMEM],
        out_specs=VMEM,
        compiler_params=params,
        cost_estimate=cost(30),
        name="clip_info",
    )(valid_count.reshape(1, 1))
    xn, xn_inverse = pl.pallas_call(
        spatial_norm,
        out_shape=(
            shape(frames_in.shape, bf16),
            shape((local_frames, patches, 1), f32),
        ),
        in_specs=[VMEM] * 2,
        out_specs=(VMEM,) * 2,
        compiler_params=params,
        cost_estimate=cost(2),
        name="spatial_norm",
    )(info, frames_in)
    part = shape((local_frames, patches, INNER), bf16)
    q, k, v, p, so = pl.pallas_call(
        spatial_attention,
        out_shape=(
            part,
            part,
            part,
            shape((local_frames, HEADS, patches, patches), bf16),
            part,
        ),
        in_specs=[VMEM] * 2,
        out_specs=(VMEM,) * 5,
        compiler_params=params,
        cost_estimate=cost(30),
        name="spatial_attention",
    )(xn, spatial_qkv)
    x1 = pl.pallas_call(
        spatial_output,
        out_shape=shape(traded, bf16),
        in_specs=[VMEM] * 3,
        out_specs=VMEM,
        compiler_params=params,
        cost_estimate=cost(2),
        name="spatial_output",
    )(frames_in, so, spatial_out)

    x1 = lax.all_to_all(x1, "frame", split_axis=0, concat_axis=0, tiled=True)
    x1 = x1.reshape(slots, share, width)
    embed_size = text_embed.shape[1]
    send, tn, inverse, tq, tk, tp, c = pl.pallas_call(
        temporal_forward,
        out_shape=(
            shape((devices, 1, embed_size + LANES), f32),
            shape((rows, width), bf16),
            shape((rows, 1), f32),
            shape((rows, INNER), bf16),
            shape((rows, INNER), bf16),
            shape((groups, HEADS, slots * GROUP, slots * GROUP), bf16),
            shape((HEADS, rows), f32),
        ),
        in_specs=[VMEM] * 8,
        out_specs=(VMEM,) * 7,
        compiler_params=params,
        cost_estimate=cost(7),
        name="temporal_forward",
    )(
        info,
        frame_time,
        x1,
        time_embed,
        temporal_qkv,
        temporal_out,
        video_proj,
        text_embed,
    )

    parts = lax.all_to_all(send, ("frame", "batch"), split_axis=0, concat_axis=0, tiled=True)
    grad_x1, loss = pl.pallas_call(
        functools.partial(temporal_backward, clips, float(slots * patches)),
        out_shape=(shape((slots, share, width), bf16), shape((GROUP, LANES), f32)),
        in_specs=[VMEM] * 12,
        out_specs=(VMEM,) * 2,
        scratch_shapes=[pltpu.VMEM((rows, width), f32)],
        compiler_params=params,
        cost_estimate=cost(8),
        name="temporal_backward",
    )(
        info,
        frame_time,
        parts,
        tn,
        inverse,
        tq,
        tk,
        tp,
        c,
        temporal_qkv,
        temporal_out,
        video_proj,
    )
    grad_x1 = lax.all_to_all(
        grad_x1.reshape(traded), "frame", split_axis=0, concat_axis=0, tiled=True
    )
    result, loss = pl.pallas_call(
        spatial_backward,
        out_shape=(shape(frames_in.shape, bf16), shape((1, 1), f32)),
        in_specs=[VMEM] * 11,
        out_specs=(HBM, HBM),
        scratch_shapes=[
            pltpu.VMEM(frames_in.shape, bf16),
            pltpu.VMEM((1, 1), f32),
            pltpu.SemaphoreType.DMA((local_frames, PIECES)),
            pltpu.SemaphoreType.DMA,
        ],
        compiler_params=params,
        cost_estimate=cost(12),
        name="spatial_backward",
    )(grad_x1, xn, xn_inverse, spatial_qkv, spatial_out, q, k, v, p, so, loss)
    return (result[None], loss[0, 0])


def solution(mesh):
    placed = (
        P("batch", "frame", None, None),
        P("batch", None),
        P("batch"),
        P(),
        P(),
        P(),
        P(),
        P(),
        P(),
        P("batch", None),
    )
    return jax.shard_map(
        per_device,
        mesh=mesh,
        in_specs=placed,
        out_specs=(P("batch", "frame", None, None), P()),
        check_vma=False,
    )
```

```python
import functools
import math

import jax
import jax.numpy as jnp
from jax import lax
from jax.experimental import pallas as pl
from jax.experimental.pallas import tpu as pltpu
from jax.sharding import PartitionSpec as P

HEADS = 8
HD = 88
INNER = HEADS * HD
LANES = 128
GROUP = 8
SPLIT = 512
PIECES = 4
EPSILON = 1e-06
SHARPNESS = 1.0 / 0.07
SCALE = 1.0 / math.sqrt(HD)
QUERY_SCALE = SCALE / math.log(2.0)
KEY_BACK = math.log(2.0)
MIB = 1024 * 1024

bf16 = jnp.bfloat16
f32 = jnp.float32
VMEM = pl.BlockSpec(memory_space=pltpu.VMEM)
HBM = pl.BlockSpec(memory_space=pltpu.HBM)


def dot_nn(left, right):
    return lax.dot_general(left, right, (((1,), (0,)), ((), ())), preferred_element_type=f32)


def dot_nt(left, right):
    return lax.dot_general(left, right, (((1,), (1,)), ((), ())), preferred_element_type=f32)


def dot_tn(left, right):
    return lax.dot_general(left, right, (((0,), (0,)), ((), ())), preferred_element_type=f32)


def split_terms(values, terms):
    parts = []
    rest = values
    for _ in range(terms):
        part = rest.astype(bf16)
        parts.append(part)
        rest = rest - part.astype(f32)
    return parts


def exact(dot, values, matrix, terms=2):
    rows = values.shape[0]
    products = dot(jnp.concatenate(split_terms(values, terms), axis=0), matrix)
    total = products[:rows]
    for term in range(1, terms):
        total = total + products[term * rows : (term + 1) * rows]
    return total


def window(head):
    first = head * HD // LANES * LANES
    last = min(-(-(head + 1) * HD // LANES) * LANES, INNER)
    return first, last, head * HD - first


def head_lanes(rows, head):
    first, last, offset = window(head)
    lane = lax.broadcasted_iota(jnp.int32, (rows, last - first), 1)
    return (lane >= offset) & (lane < offset + HD)


def keep_head(values, head):
    return jnp.where(head_lanes(values.shape[0], head), values, jnp.zeros_like(values))


def merge_heads(products):
    tiles = []
    for start in range(0, INNER, LANES):
        width = min(LANES, INNER - start)
        tile = None
        for head in range(HEADS):
            first, last, offset = window(head)
            if first <= start < last:
                piece = products[head][:, start - first : start - first + width]
                if tile is None:
                    tile = piece
                else:
                    lane = lax.broadcasted_iota(jnp.int32, piece.shape, 1)
                    tile = jnp.where(lane >= head * HD - start, piece, tile)
        tiles.append(tile)
    return jnp.concatenate(tiles, axis=1)


def normalize(values):
    center = values - jnp.mean(values, axis=-1, keepdims=True)
    spread = jnp.mean(center * center, axis=-1, keepdims=True)
    inverse = lax.rsqrt(spread + EPSILON)
    return center * inverse, inverse


def normalize_back(grad, normed, inverse):
    return inverse * (
        grad
        - jnp.mean(grad, axis=-1, keepdims=True)
        - normed * jnp.mean(grad * normed, axis=-1, keepdims=True)
    )


def clip_info(patches, count_ref, info_ref):
    count = count_ref[...].astype(f32)
    info_ref[0:1, :] = jnp.broadcast_to(count, (1, info_ref.shape[1]))
    scale = 1.0 / (count * float(patches))
    info_ref[1:2, :] = jnp.broadcast_to(scale, (1, info_ref.shape[1]))


def spatial_norm(info_ref, tok_ref, xn_ref, inverse_ref):
    del info_ref
    for frame in range(tok_ref.shape[0]):
        normed, inverse = normalize(tok_ref[frame].astype(f32))
        xn_ref[frame] = normed.astype(bf16)
        inverse_ref[frame] = inverse


def spatial_attention(xn_ref, qkv_ref, q_ref, k_ref, v_ref, p_ref, so_ref):
    for frame in range(xn_ref.shape[0]):
        packed = dot_nt(xn_ref[frame], qkv_ref[...])
        q_ref[frame] = (packed[:, :INNER] * QUERY_SCALE).astype(bf16)
        k_ref[frame] = packed[:, INNER : 2 * INNER].astype(bf16)
        v_ref[frame] = packed[:, 2 * INNER :].astype(bf16)
        scores = []
        for head in range(HEADS):
            first, last, _ = window(head)
            query = keep_head(q_ref[frame, :, first:last], head)
            scores.append(dot_nt(query, k_ref[frame, :, first:last]))
        for head in range(HEADS):
            raised = jnp.exp2(scores[head])
            weights = raised * (1.0 / jnp.sum(raised, axis=-1, keepdims=True))
            p_ref[frame, head] = weights.astype(bf16)
        mixed = []
        for head in range(HEADS):
            first, last, _ = window(head)
            mixed.append(dot_nn(p_ref[frame, head], v_ref[frame, :, first:last]))
        so_ref[frame] = merge_heads(mixed).astype(bf16)


def spatial_output(tok_ref, so_ref, out_ref, x1_ref):
    frames, patches, width = tok_ref.shape
    owners = x1_ref.shape[0]
    share = patches // owners
    for frame in range(frames):
        update = dot_nn(so_ref[frame], out_ref[...])
        x1 = (tok_ref[frame].astype(f32) + update).astype(bf16)
        own = slice(frame * share, (frame + 1) * share)
        x1_ref[:, own, :] = x1.reshape(owners, share, width)


def spatial_backward(
    grad_ref,
    xn_ref,
    inverse_ref,
    qkv_ref,
    out_ref,
    q_ref,
    k_ref,
    v_ref,
    p_ref,
    so_ref,
    loss_ref,
    result_hbm,
    loss_hbm,
    result_ref,
    loss_held_ref,
    result_sem,
    loss_sem,
):
    loss_held_ref[...] = loss_ref[:1, :1]
    loss_copy = pltpu.make_async_copy(loss_held_ref, loss_hbm, loss_sem)
    loss_copy.start()
    frames, patches, width = xn_ref.shape
    owners = grad_ref.shape[0]
    share = patches // owners
    copies = []

    def rows_of(frame):
        return slice(frame * share, (frame + 1) * share)

    def first_products(frame):
        grad_x1 = grad_ref[:, rows_of(frame), :].reshape(patches, width)
        grad_so = dot_nt(grad_x1, out_ref[...]).astype(bf16)
        dv, grad_weights, inner = [], [], []
        for head in range(HEADS):
            first, last, _ = window(head)
            dv.append(dot_tn(p_ref[frame, head], grad_so[:, first:last]))
        for head in range(HEADS):
            first, last, _ = window(head)
            grad_head = keep_head(grad_so[:, first:last], head)
            along = grad_head.astype(f32) * so_ref[frame, :, first:last].astype(f32)
            inner.append(jnp.sum(along, axis=-1, keepdims=True))
            grad_weights.append(dot_nt(grad_head, v_ref[frame, :, first:last]))
        return merge_heads(dv).astype(bf16), grad_weights, inner

    def score_grads(frame, grad_weights, inner):
        grad_scores = []
        for head in range(HEADS):
            weights = p_ref[frame, head].astype(f32)
            grad_scores.append((weights * (grad_weights[head] - inner[head])).astype(bf16))
        return grad_scores

    def second_products(frame, grad_scores):
        dq, dk = [], []
        for head in range(HEADS):
            first, last, _ = window(head)
            dq.append(dot_nn(grad_scores[head], k_ref[frame, :, first:last]))
            dk.append(dot_tn(grad_scores[head], q_ref[frame, :, first:last]))
        return (merge_heads(dq) * SCALE).astype(bf16), (merge_heads(dk) * KEY_BACK).astype(bf16)

    def finish(frame, grad_xn):
        for piece in range(PIECES):
            size = patches // PIECES
            at = slice(piece * size, (piece + 1) * size)
            back = normalize_back(
                grad_xn[at], xn_ref[frame, at].astype(f32), inverse_ref[frame, at]
            )
            held = slice(piece * owners // PIECES, (piece + 1) * owners // PIECES)
            grad_x1 = grad_ref[held, rows_of(frame), :].reshape(size, width)
            result_ref[frame, at] = (grad_x1.astype(f32) + back).astype(bf16)
            rows = pl.ds(piece * size, size)
            copy = pltpu.make_async_copy(
                result_ref.at[frame, rows],
                result_hbm.at[frame, rows],
                result_sem.at[frame, piece],
            )
            copy.start()
            copies.append(copy)

    waiting = first_products(0)
    before = None
    for frame in range(frames):
        dv, grad_weights, inner = waiting
        grad_scores = score_grads(frame, grad_weights, inner)
        if frame + 1 < frames:
            waiting = first_products(frame + 1)
        dq, dk = second_products(frame, grad_scores)
        if before is not None:
            finish(frame - 1, before)
        before = dot_nn(dq, qkv_ref[:INNER, :])
        before += dot_nn(dk, qkv_ref[INNER : 2 * INNER, :])
        before += dot_nn(dv, qkv_ref[2 * INNER :, :])
    finish(frames - 1, before)
    for copy in copies + [loss_copy]:
        copy.wait()


def slot_columns(valid, rows):
    slots = valid.shape[1]
    row_slot = lax.broadcasted_iota(jnp.int32, (rows, slots), 0) // GROUP
    slot = lax.broadcasted_iota(jnp.int32, (rows, slots), 1)
    column = jnp.sum(jnp.where(row_slot == slot, valid, 0.0), axis=1, keepdims=True)
    return column


def temporal_forward(
    info_ref,
    times_ref,
    x1_ref,
    embed_ref,
    qkv_ref,
    out_ref,
    proj_ref,
    text_ref,
    send_ref,
    tn_ref,
    inverse_ref,
    q_ref,
    k_ref,
    p_ref,
    c_ref,
):
    slots, share, width = x1_ref.shape
    groups = share // GROUP
    rows = slots * GROUP
    times = times_ref[...].astype(f32)
    valid = jnp.where(times < info_ref[0:1, :slots], 1.0, 0.0)
    time = lax.broadcasted_iota(jnp.int32, (embed_ref.shape[0], slots), 0).astype(f32)
    lookup = jnp.where(time == times, 1.0, 0.0).astype(bf16)
    added = None
    for part in split_terms(embed_ref[...], 3):
        term = dot_tn(lookup, part)
        added = term if added is None else added + term
    valid_column = slot_columns(valid, rows)
    slot_index = lax.broadcasted_iota(jnp.int32, (slots, slots), 0)
    own_slot = slot_index == lax.broadcasted_iota(jnp.int32, (slots, slots), 1)
    valid_slots = jnp.sum(jnp.where(own_slot, valid, 0.0), axis=1, keepdims=True)
    chunk = 8
    all_rows = slots * share
    row_slot = lax.broadcasted_iota(jnp.int32, (slots, all_rows), 1) // share
    own_row = lax.broadcasted_iota(jnp.int32, (slots, all_rows), 0) == row_slot
    spread_rows = jnp.where(own_row, 1.0, 0.0).astype(bf16)
    valid_rows = jnp.broadcast_to(valid, (GROUP, slots)).astype(bf16)
    row_valid = dot_nn(valid_rows, spread_rows).astype(bf16)
    pooled = dot_nn(row_valid, x1_ref[...].reshape(all_rows, width))[:1]
    for slot in range(0, slots, GROUP):
        kept = valid_slots[slot : slot + GROUP] * added[slot : slot + GROUP]
        pooled = pooled + float(share) * jnp.sum(kept, axis=0, keepdims=True)
    for start in range(0, slots, chunk):
        y = x1_ref[start : start + chunk].astype(f32) + added[start : start + chunk][:, None, :]
        normed, inverse = normalize(y)
        for group in range(groups):
            own = slice(group * GROUP, (group + 1) * GROUP)
            at = pl.ds(group * rows + start * GROUP, chunk * GROUP)
            tn_ref[at, :] = normed[:, own, :].reshape(chunk * GROUP, width).astype(bf16)
            inverse_ref[at, :] = inverse[:, own, :].reshape(chunk * GROUP, 1)
    row_index = lax.broadcasted_iota(jnp.int32, (rows, rows), 0)
    column_index = lax.broadcasted_iota(jnp.int32, (rows, rows), 1)
    spread = jnp.where(
        lax.broadcasted_iota(jnp.int32, (slots, rows), 0)
        == lax.broadcasted_iota(jnp.int32, (slots, rows), 1) // GROUP,
        1.0,
        0.0,
    ).astype(bf16)
    key_valid = dot_nn(jnp.broadcast_to(valid, (GROUP, slots)).astype(bf16), spread)[:1]
    allowed = (row_index % GROUP == column_index % GROUP) & (key_valid > 0.5)
    for group in range(groups):
        at = pl.ds(group * rows, rows)
        packed = dot_nt(tn_ref[at, :], qkv_ref[: 2 * INNER, :])
        q_ref[at, :] = (packed[:, :INNER] * QUERY_SCALE).astype(bf16)
        k_ref[at, :] = packed[:, INNER:].astype(bf16)
        scores = []
        for head in range(HEADS):
            first, last, _ = window(head)
            query = keep_head(q_ref[at, first:last], head)
            scores.append(dot_nt(query, k_ref[at, first:last]))
        for head in range(HEADS):
            raised = jnp.where(allowed, jnp.exp2(scores[head]), 0.0)
            weights = raised * (valid_column / jnp.sum(raised, axis=-1, keepdims=True))
            p_ref[group, head] = weights.astype(bf16)
            c_ref[head : head + 1, at] = jnp.sum(weights, axis=0, keepdims=True)
    gathered = exact(dot_nn, c_ref[...], tn_ref[...])
    mixed_all = exact(dot_nt, gathered, qkv_ref[2 * INNER :, :])
    lane = lax.broadcasted_iota(jnp.int32, mixed_all.shape, 1)
    head_row = lax.broadcasted_iota(jnp.int32, mixed_all.shape, 0)
    own_lane = (lane >= head_row * HD) & (lane < head_row * HD + HD)
    mixed = jnp.sum(jnp.where(own_lane, mixed_all, 0.0), axis=0, keepdims=True)
    feature = pooled + exact(dot_nn, jnp.broadcast_to(mixed, (GROUP, INNER)), out_ref[...])[:1]
    z = exact(dot_nn, jnp.broadcast_to(feature, (GROUP, width)), proj_ref[...])[:1]
    z = z * info_ref[1:2, :1]
    embed_size = z.shape[1]
    send_ref[:, :, :embed_size] = jnp.broadcast_to(
        z[None], (send_ref.shape[0], 1, embed_size)
    )
    tiles = embed_size // LANES
    own_tile = lax.axis_index("frame") // (lax.axis_size("frame") // tiles)
    piece = jnp.zeros((1, LANES), f32)
    for tile in range(tiles):
        held = text_ref[:, tile * LANES : (tile + 1) * LANES]
        piece = jnp.where(own_tile == tile, held, piece)
    send_ref[:, :, embed_size:] = jnp.broadcast_to(piece[None], (send_ref.shape[0], 1, LANES))


def unit_rows(matrix):
    inverse = lax.rsqrt(jnp.sum(matrix * matrix, axis=-1, keepdims=True) + EPSILON)
    return matrix * inverse, inverse


def temporal_backward(
    batch,
    cotangent,
    info_ref,
    times_ref,
    parts_ref,
    tn_ref,
    inverse_ref,
    q_ref,
    k_ref,
    p_ref,
    c_ref,
    qkv_ref,
    out_ref,
    proj_ref,
    grad_ref,
    loss_ref,
    dtn_ref,
):
    slots, share, width = grad_ref.shape
    groups = share // GROUP
    rows = slots * GROUP
    clips = batch
    per_clip = parts_ref.shape[0] // clips
    embed_size = proj_ref.shape[1]
    parts = parts_ref[:, 0, :].reshape(per_clip, clips, parts_ref.shape[2])
    z = jnp.sum(parts[:, :, :embed_size], axis=0)
    tiles = embed_size // LANES
    text = jnp.concatenate(
        [parts[i * (per_clip // tiles), :, embed_size:] for i in range(tiles)], axis=1
    )
    e, inverse_z = unit_rows(z)
    u, _ = unit_rows(text)
    column = lax.broadcasted_iota(jnp.int32, (clips, clips), 1)
    logits = jnp.zeros((clips, clips), f32)
    for j in range(clips):
        product = jnp.sum(e * u[j : j + 1], axis=1, keepdims=True) * SHARPNESS
        logits = jnp.where(column == j, product, logits)
    raised = jnp.exp(logits)
    row_total = jnp.sum(raised, axis=1, keepdims=True)
    column_total = jnp.sum(raised, axis=0, keepdims=True)
    diagonal = lax.broadcasted_iota(jnp.int32, logits.shape, 0) == lax.broadcasted_iota(
        jnp.int32, logits.shape, 1
    )
    loss = (
        0.5 * jnp.sum(jnp.log(row_total), axis=0, keepdims=True)
        + 0.5 * jnp.sum(jnp.log(column_total), axis=1, keepdims=True)
        - jnp.sum(jnp.sum(jnp.where(diagonal, logits, 0.0), axis=1, keepdims=True), axis=0, keepdims=True)
    )
    loss_ref[...] = jnp.broadcast_to(loss, loss_ref.shape)
    shares = 0.5 * (raised / row_total + raised / column_total) - jnp.where(diagonal, 1.0, 0.0)
    shares = shares * (cotangent * SHARPNESS)
    grad_e = shares[:, 0:1] * u[0:1]
    for j in range(1, clips):
        grad_e = grad_e + shares[:, j : j + 1] * u[j : j + 1]
    grad_z = inverse_z * (grad_e - e * jnp.sum(e * grad_e, axis=-1, keepdims=True))
    own = lax.broadcasted_iota(jnp.int32, grad_z.shape, 0) == lax.axis_index("batch")
    grad_own = jnp.sum(jnp.where(own, grad_z, 0.0), axis=0, keepdims=True)
    grad_own = grad_own * info_ref[1:2, :1]
    grad_feature = exact(dot_nt, jnp.broadcast_to(grad_own, grad_z.shape), proj_ref[...])
    grad_mixed = exact(dot_nt, grad_feature, out_ref[...])
    lane = lax.broadcasted_iota(jnp.int32, grad_mixed.shape, 1)
    head_row = lax.broadcasted_iota(jnp.int32, grad_mixed.shape, 0)
    own_lane = (lane >= head_row * HD) & (lane < head_row * HD + HD)
    value_grad = exact(dot_nn, jnp.where(own_lane, grad_mixed, 0.0), qkv_ref[2 * INNER :, :])
    high, low = split_terms(value_grad, 2)
    scores_grad = exact(dot_nt, value_grad, tn_ref[...])
    c_high, c_low = split_terms(c_ref[...], 2)
    times = times_ref[...].astype(f32)
    valid = jnp.where(times < info_ref[0:1, :slots], 1.0, 0.0)
    valid_column = slot_columns(valid, rows)
    for group in range(groups):
        at = pl.ds(group * rows, rows)
        grad_scores = []
        for head in range(HEADS):
            weights = p_ref[group, head].astype(f32)
            along = scores_grad[head : head + 1, group * rows : (group + 1) * rows]
            inner = jnp.sum(weights * along, axis=-1, keepdims=True)
            grad_scores.append((weights * (along - inner)).astype(bf16))
        dq, dk = [], []
        for head in range(HEADS):
            first, last, _ = window(head)
            dq.append(dot_nn(grad_scores[head], k_ref[at, first:last]))
        for head in range(HEADS):
            first, last, _ = window(head)
            dk.append(dot_tn(grad_scores[head], q_ref[at, first:last]))
        own = slice(group * rows, (group + 1) * rows)
        weights_c = jnp.concatenate([c_high[:, own], c_high[:, own], c_low[:, own]], axis=0)
        value_rows = jnp.concatenate([high, low, high], axis=0)
        grad_tn = dot_nn((merge_heads(dq) * SCALE).astype(bf16), qkv_ref[:INNER, :])
        dk = (merge_heads(dk) * KEY_BACK).astype(bf16)
        grad_tn += dot_nn(dk[:, :SPLIT], qkv_ref[INNER : INNER + SPLIT, :])
        last = jnp.concatenate([dk[:, SPLIT:], weights_c.astype(f32).T.astype(bf16)], axis=1)
        rest_rows = jnp.concatenate([qkv_ref[INNER + SPLIT : 2 * INNER, :], value_rows], axis=0)
        dtn_ref[at, :] = grad_tn + dot_nn(last, rest_rows)
    chunk = 8
    for start in range(0, slots, chunk):
        pieces = []
        for group in range(groups):
            at = pl.ds(group * rows + start * GROUP, chunk * GROUP)
            back = normalize_back(dtn_ref[at, :], tn_ref[at, :].astype(f32), inverse_ref[at, :])
            back = (
                back
                + valid_column[start * GROUP : (start + chunk) * GROUP] * grad_feature[:1]
            )
            pieces.append(back.reshape(chunk, 1, GROUP, width))
        joined = jnp.concatenate(pieces, axis=1).reshape(chunk, share, width)
        grad_ref[start : start + chunk] = joined.astype(bf16)


def cost(microseconds):
    return pl.CostEstimate(flops=microseconds * 10**9, bytes_accessed=0, transcendentals=0)


def per_device(
    tokens,
    frame_time,
    valid_count,
    spatial_qkv,
    spatial_out,
    temporal_qkv,
    temporal_out,
    time_embed,
    video_proj,
    text_embed,
):
    frames_in = tokens[0]
    local_frames, patches, width = frames_in.shape
    owners = lax.axis_size("frame")
    clips = lax.axis_size("batch")
    devices = owners * clips
    share = patches // owners
    slots = owners * local_frames
    groups = share // GROUP
    rows = slots * share
    shape = jax.ShapeDtypeStruct
    traded = (owners, local_frames * share, width)
    params = pltpu.CompilerParams(vmem_limit_bytes=20 * MIB)
    spatial_qkv = spatial_qkv.T
    temporal_qkv = temporal_qkv.T
    info = pl.pallas_call(
        functools.partial(clip_info, patches),
        out_shape=shape((GROUP, LANES), f32),
        in_specs=[VMEM],
        out_specs=VMEM,
        compiler_params=params,
        cost_estimate=cost(30),
        name="clip_info",
    )(valid_count.reshape(1, 1))
    xn, xn_inverse = pl.pallas_call(
        spatial_norm,
        out_shape=(
            shape(frames_in.shape, bf16),
            shape((local_frames, patches, 1), f32),
        ),
        in_specs=[VMEM] * 2,
        out_specs=(VMEM,) * 2,
        compiler_params=params,
        cost_estimate=cost(2),
        name="spatial_norm",
    )(info, frames_in)
    part = shape((local_frames, patches, INNER), bf16)
    q, k, v, p, so = pl.pallas_call(
        spatial_attention,
        out_shape=(
            part,
            part,
            part,
            shape((local_frames, HEADS, patches, patches), bf16),
            part,
        ),
        in_specs=[VMEM] * 2,
        out_specs=(VMEM,) * 5,
        compiler_params=params,
        cost_estimate=cost(30),
        name="spatial_attention",
    )(xn, spatial_qkv)
    x1 = pl.pallas_call(
        spatial_output,
        out_shape=shape(traded, bf16),
        in_specs=[VMEM] * 3,
        out_specs=VMEM,
        compiler_params=params,
        cost_estimate=cost(2),
        name="spatial_output",
    )(frames_in, so, spatial_out)

    x1 = lax.all_to_all(x1, "frame", split_axis=0, concat_axis=0, tiled=True)
    x1 = x1.reshape(slots, share, width)
    embed_size = text_embed.shape[1]
    send, tn, inverse, tq, tk, tp, c = pl.pallas_call(
        temporal_forward,
        out_shape=(
            shape((devices, 1, embed_size + LANES), f32),
            shape((rows, width), bf16),
            shape((rows, 1), f32),
            shape((rows, INNER), bf16),
            shape((rows, INNER), bf16),
            shape((groups, HEADS, slots * GROUP, slots * GROUP), bf16),
            shape((HEADS, rows), f32),
        ),
        in_specs=[VMEM] * 8,
        out_specs=(VMEM,) * 7,
        compiler_params=params,
        cost_estimate=cost(7),
        name="temporal_forward",
    )(
        info,
        frame_time,
        x1,
        time_embed,
        temporal_qkv,
        temporal_out,
        video_proj,
        text_embed,
    )

    parts = lax.all_to_all(send, ("frame", "batch"), split_axis=0, concat_axis=0, tiled=True)
    grad_x1, loss = pl.pallas_call(
        functools.partial(temporal_backward, clips, float(slots * patches)),
        out_shape=(shape((slots, share, width), bf16), shape((GROUP, LANES), f32)),
        in_specs=[VMEM] * 12,
        out_specs=(VMEM,) * 2,
        scratch_shapes=[pltpu.VMEM((rows, width), f32)],
        compiler_params=params,
        cost_estimate=cost(8),
        name="temporal_backward",
    )(
        info,
        frame_time,
        parts,
        tn,
        inverse,
        tq,
        tk,
        tp,
        c,
        temporal_qkv,
        temporal_out,
        video_proj,
    )
    grad_x1 = lax.all_to_all(
        grad_x1.reshape(traded), "frame", split_axis=0, concat_axis=0, tiled=True
    )
    result, loss = pl.pallas_call(
        spatial_backward,
        out_shape=(shape(frames_in.shape, bf16), shape((1, 1), f32)),
        in_specs=[VMEM] * 11,
        out_specs=(HBM, HBM),
        scratch_shapes=[
            pltpu.VMEM(frames_in.shape, bf16),
            pltpu.VMEM((1, 1), f32),
            pltpu.SemaphoreType.DMA((local_frames, PIECES)),
            pltpu.SemaphoreType.DMA,
        ],
        compiler_params=params,
        cost_estimate=cost(12),
        name="spatial_backward",
    )(grad_x1, xn, xn_inverse, spatial_qkv, spatial_out, q, k, v, p, so, loss)
    return (result[None], loss[0, 0])


def solution(mesh):
    placed = (
        P("batch", "frame", None, None),
        P("batch", None),
        P("batch"),
        P(),
        P(),
        P(),
        P(),
        P(),
        P(),
        P("batch", None),
    )
    return jax.shard_map(
        per_device,
        mesh=mesh,
        in_specs=placed,
        out_specs=(P("batch", "frame", None, None), P()),
        check_vma=False,
    )
```
